32 devices in a mesh: dp: 8 (over z, x), mp: 4 (over y, core).
Axes of the slice: x: 2, y: 2, z: 4, core: 2. Of those that a mesh axis runs over, the one named last changes fastest.
Arguments:
- frames: bfloat16 [2048, 2, 16, 256], P('dp', None, None, 'mp')
- cache: bfloat16 [2048, 2, 16, 256], P('dp', None, None, 'mp'), may hold values from -6 to 6
- group_offset: int32 [128], replicated, may hold values from 0 to 7, as said below
- cache_offset: int32 [128], replicated, may hold values from 0 to 7, as said below
- cache_group: int32 [128], replicated, may hold values from 0 to 127, each once
- group_rows: int32 [8, 128], P('dp'), may hold values from 1 to 2, 192 in all within a row
- cache_live: int32 [1024], P('dp'), may hold values 0 or 1
- temporal_weight: bfloat16 [3, 256, 512], P(None, None, 'mp')
- spatial_weight: bfloat16 [3, 512, 512], P(None, None, 'mp'), may hold values from -0.15625 to 0.15625
- norm_gain: bfloat16 [512], P('mp'), may hold values from 0.25 to 1.75
Outputs:
- latents: bfloat16 [2048, 2, 16, 512], P('dp', None, None, 'mp')
The draws below stay inside these ranges and needn't reach their ends.
Inputs may be any that keep to these rules, and one draw needn't show every extreme that they name: group_offset[g] equals group_offset[g2] exactly when g - g2 is a multiple of 8. cache_offset[h] equals cache_offset[h2] exactly when h - h2 is a multiple of 8.
All inputs are finite; a program needn't handle non-finite values. No bound on the sum of `cache_live` on one device may be relied on, other than what follows from the above.
Results may differ from the reference program's by a relative error of at most 0.0026.
Values may be sent and summed in bfloat16 or wider, within the bound.
No kernel may reach another device: no remote copies, remote signals or barrier semaphores. Data moves between devices by JAX's collectives and lax.ppermute only.
A program may use at most 128 MiB of HBM per device.

```python
import math
import jax
import jax.numpy as jnp
import numpy as np
from jax import lax

C_IN = 256
C = 512
W = 16
TS = 2
K = 3
P_SIZE = 2
G = 128
N_DP = 8


def draw_frames(key, part):
    first, second = jax.random.split(key, 2)
    shape = (N_DP * G * P_SIZE, TS, W, C_IN)
    base = jnp.clip(jax.random.normal(first, shape, jnp.float32), -6.0, 6.0)
    scale = 10.0 ** jax.random.uniform(second, (N_DP * G * P_SIZE, TS, W, 1), jnp.float32, -0.5, 0.5)
    return (base * scale).astype(jnp.bfloat16)


def draw_temporal_weight(key, part):
    first, second = jax.random.split(key)
    base = jnp.clip(jax.random.normal(first, (K, C_IN, C), jnp.float32), -6.0, 6.0) * (K * C_IN) ** (-0.5)
    column = jnp.arange(C, dtype=jnp.float32) / C - 0.5
    rough = jnp.exp(jax.random.uniform(second, (1, 1, C), jnp.float32, -0.4, 0.4))
    return (base * (10.0 ** column)[None, None, :] * rough).astype(jnp.bfloat16)


def offset_table(key):
    first, second = jax.random.split(key)
    values = jnp.arange(N_DP, dtype=jnp.int32)
    scores = jax.random.permutation(first, N_DP).astype(jnp.int32)
    forced = (values == 1) | (values == N_DP // 2)
    scores = jnp.where(forced, scores - 2 * N_DP, scores)
    ordered = values[jnp.argsort(scores, stable=True)]
    used = min(G, N_DP)
    leading = ordered[:used]
    placed = leading[jax.random.permutation(second, used).astype(jnp.int32)]
    return placed[jnp.arange(G, dtype=jnp.int32) % used].astype(jnp.int32)


def draw_group_offset(key, part):
    return offset_table(jax.random.fold_in(key, 11))


def draw_cache_offset(key, part):
    return offset_table(jax.random.fold_in(key, 23))


def place_ends(drawn, stream_key, low, top_value):
    longest = drawn.shape.index(max(drawn.shape))
    spots = []
    for shift in (0, 1):
        where = [jax.random.randint(jax.random.fold_in(stream_key, axis), (), 0, length) for axis, length in enumerate(drawn.shape)]
        where[longest] = (where[longest] + shift) % drawn.shape[longest]
        spots.append(tuple(where))
    return drawn.at[spots[0]].set(low).at[spots[1]].set(top_value)


def levels(own_key, extent, cuts, least, largest):
    gain, own = 1.0, jax.random.fold_in(own_key, 6)
    for position, shards_of in cuts:
        steps = jnp.exp(jax.random.uniform(jax.random.fold_in(own, position), (shards_of,), jnp.float32, least / len(cuts), largest / len(cuts)))
        gain = gain * jnp.repeat(steps, extent[position] // shards_of).reshape([-1 if axis == position else 1 for axis in range(len(extent))])
    return gain


def length_profile(count, total, most, lean):
    loads = [(1 << 20) // math.isqrt(rank ** lean) + 1 for rank in range(2, count + 1)]
    spare, holding = total - most - (count - 1), [1] * (count - 1)
    while spare > 0:
        free = [i for i in range(count - 1) if holding[i] < most]
        pool, remaining = sum([loads[i] for i in free]), spare
        for i in free:
            extra = min(most - holding[i], max(1, remaining * loads[i] // pool), spare)
            holding[i] = holding[i] + extra
            spare = spare - extra
    return np.array([most] + holding)


def uneven_parts(rng, number_of, total, bound, slope):
    if number_of == 2:
        one = jax.random.randint(rng, (), max(1, total - bound), min(bound, total - 1) + 1)
        return jnp.stack([one, total - one])
    tallies = jnp.asarray(length_profile(number_of, total, bound, slope), jnp.int32)
    couples = (number_of - 1) // 2
    source_of, taker = tallies[1:1 + 2 * couples:2], tallies[2:2 + 2 * couples:2]
    margin = jnp.minimum(source_of - 1, bound - taker)
    passed = jax.random.randint(jax.random.fold_in(rng, 1), (couples,), 0, 1 << 20) % (margin + 1)
    tallies = tallies.at[1:1 + 2 * couples:2].set(source_of - passed).at[2:2 + 2 * couples:2].set(taker + passed)
    return tallies[jax.random.permutation(jax.random.fold_in(rng, 2), number_of)]


def scatter_about(own_key, extent, spread, limit, cuts=(), kind=jnp.bfloat16):
    array = spread * jax.random.normal(own_key, extent, jnp.float32)
    if cuts:
        array = array * levels(own_key, extent, cuts, -0.22, 0.18)
    return jnp.clip(array, -limit, limit).astype(kind)


def setup_inputs(seed: int = 0) -> dict:
    seeds = jax.random.split(jax.random.key(seed), 11)
    frames = draw_frames(jax.random.fold_in(seeds[10], 71), 0)
    cache = scatter_about(seeds[1], (N_DP * G * P_SIZE, K - 1, W, C_IN), 1.0, 6.0, ((0, 8), (3, 4)))
    group_offset = draw_group_offset(jax.random.fold_in(seeds[10], 71), 0)
    cache_offset = draw_cache_offset(jax.random.fold_in(seeds[10], 71), 0)
    cache_group = jax.random.permutation(seeds[4], G).astype(jnp.int32)
    group_rows = jax.vmap(lambda own: uneven_parts(own, G, (P_SIZE + 1) * G // 2, P_SIZE, 1))(jax.random.split(seeds[5], N_DP)).reshape((N_DP, G)).astype(jnp.int32)
    cache_live = place_ends((jax.random.randint(seeds[6], (N_DP * G,), 0, 4) < 3).astype(jnp.int32), jax.random.fold_in(seeds[6], 1), 0, 1)
    temporal_weight = draw_temporal_weight(jax.random.fold_in(seeds[10], 71), 0)
    spatial_weight = scatter_about(seeds[8], (3, C, C), (3 * C) ** -0.5, 0.15625, ((2, 4),))
    norm_gain = jnp.clip(1.0 + 0.15 * jax.random.normal(seeds[9], (C,), jnp.float32), 0.25, 1.75).astype(jnp.bfloat16)
    return dict(frames=frames, cache=cache, group_offset=group_offset, cache_offset=cache_offset, cache_group=cache_group, group_rows=group_rows, cache_live=cache_live, temporal_weight=temporal_weight, spatial_weight=spatial_weight, norm_gain=norm_gain)


def reference(frames, cache, group_offset, cache_offset, cache_group, group_rows, cache_live, temporal_weight, spatial_weight, norm_gain):
    stored = frames.reshape(N_DP, G, P_SIZE, TS, W, C_IN)
    carried_all = cache.reshape(N_DP, G, P_SIZE, K - 1, W, C_IN)
    live_all = cache_live.reshape(N_DP, G)
    owner_ids = jnp.arange(N_DP, dtype=jnp.int32)
    group_ids = jnp.arange(G, dtype=jnp.int32)
    inverse = lax.optimization_barrier(jnp.sum(group_ids[:, None] * (cache_group[:, None] == group_ids[None, :]).astype(jnp.int32), axis=0)).astype(jnp.int32)
    sources = (owner_ids[:, None] - group_offset[None, :]) % N_DP
    previous = (owner_ids[:, None] - cache_offset[inverse][None, :]) % N_DP
    time_weight = temporal_weight.astype(jnp.float32)
    space_weight = spatial_weight.astype(jnp.float32)
    gain_full = norm_gain.astype(jnp.float32)

    def encode(owner):
        source_row = sources[owner]
        prev_row = previous[owner]
        rows = stored[source_row, group_ids]
        counts = group_rows[source_row, group_ids]
        carried = carried_all[prev_row, inverse]
        flags = live_all[prev_row, inverse]
        carried = jnp.where(flags[:, None, None, None, None] > 0, carried, jnp.zeros_like(carried))
        sequence = jnp.concatenate([carried, rows], axis=2).astype(jnp.float32)
        conv_time = jnp.zeros((G, P_SIZE, TS, W, C), jnp.float32)
        for tap_index in range(K):
            window = sequence[:, :, K - 1 - tap_index:K - 1 - tap_index + TS]
            conv_time = conv_time + jnp.einsum('gptwc,cd->gptwd', window, time_weight[tap_index])
        mean_square = lax.optimization_barrier(jnp.mean(conv_time * conv_time, axis=-1, keepdims=True))
        activated = jax.nn.silu(conv_time * lax.rsqrt(mean_square + 1e-06) * gain_full).astype(jnp.bfloat16)
        padded = jnp.pad(activated, ((0, 0), (0, 0), (0, 0), (1, 1), (0, 0))).astype(jnp.float32)
        conv_space = jnp.zeros((G, P_SIZE, TS, W, C), jnp.float32)
        for tap_index in range(3):
            conv_space = conv_space + jnp.einsum('gptwc,cd->gptwd', padded[:, :, :, tap_index:tap_index + W], space_weight[tap_index])
        live_rows = jnp.arange(P_SIZE, dtype=jnp.int32)[None, :] < counts[:, None]
        total = jnp.where(live_rows[:, :, None, None, None], conv_time + conv_space, 0.0)
        return total.astype(jnp.bfloat16)
    encoded = lax.map(encode, owner_ids)
    return encoded.reshape(N_DP * G * P_SIZE, TS, W, C)
```

```python
import functools

import jax
import jax.numpy as jnp
from jax import lax
from jax.experimental import pallas as pl
from jax.experimental.pallas import tpu as pltpu
from jax.sharding import PartitionSpec as P


def temporal_conv(sequence, weight_part, span_steps):
    taps = weight_part.shape[0]
    windows = [
        sequence[:, taps - 1 - tap_index : taps - 1 - tap_index + span_steps]
        for tap_index in range(taps)
    ]
    joined = jnp.concatenate(windows, axis=3)
    flat_weight = weight_part.reshape((taps * weight_part.shape[1], weight_part.shape[2]))
    return jnp.einsum("rtwc,cd->rtwd", joined, flat_weight, preferred_element_type=jnp.float32)


def spatial_conv(activated, weight_part):
    width = activated.shape[2]
    padded = jnp.pad(activated, ((0, 0), (0, 0), (1, 1), (0, 0)))
    joined = jnp.concatenate(
        [padded[:, :, tap_index : tap_index + width] for tap_index in range(3)], axis=3
    )
    flat_weight = weight_part.reshape((3 * weight_part.shape[1], weight_part.shape[2]))
    return jnp.einsum("rtwc,cd->rtwd", joined, flat_weight, preferred_element_type=jnp.float32)


def to_slots(values, slot_index, owner_count, per_pair):
    buffer = (
        jnp.zeros((owner_count * per_pair,) + values.shape[1:], values.dtype)
        .at[slot_index]
        .set(values)
    )
    return buffer.reshape((owner_count, per_pair) + values.shape[1:])


def plain_local(
    frames,
    cache,
    group_offset,
    cache_offset,
    cache_group,
    group_rows,
    cache_live,
    temporal_weight,
    spatial_weight,
    norm_gain,
):
    owner_count = lax.axis_size("dp")
    my_rank = lax.axis_index("dp")
    groups = group_offset.shape[0]
    pair_rows = frames.shape[0] // groups
    span_steps = frames.shape[1]
    per_pair = (groups + owner_count - 1) // owner_count
    group_index = jnp.arange(groups, dtype=jnp.int32)
    slot_level = group_index // owner_count
    grouped = frames.reshape((groups, pair_rows) + frames.shape[1:])
    counts = group_rows.reshape(groups)
    send_slot = (my_rank + group_offset) % owner_count * per_pair + slot_level
    got_rows, got_counts = (
        lax.all_to_all(
            to_slots(grouped, send_slot, owner_count, per_pair),
            "dp",
            split_axis=0,
            concat_axis=0,
            tiled=True,
        ),
        lax.all_to_all(
            to_slots(counts, send_slot, owner_count, per_pair),
            "dp",
            split_axis=0,
            concat_axis=0,
            tiled=True,
        ),
    )
    take_slot = (my_rank - group_offset) % owner_count * per_pair + slot_level
    own_rows = got_rows.reshape((owner_count * per_pair,) + grouped.shape[1:])[take_slot]
    own_counts = got_counts.reshape(owner_count * per_pair)[take_slot]
    cache_grouped = cache.reshape((groups, pair_rows) + cache.shape[1:])
    cache_send = (my_rank + cache_offset) % owner_count * per_pair + slot_level
    got_cache, got_flags = (
        lax.all_to_all(
            to_slots(cache_grouped, cache_send, owner_count, per_pair),
            "dp",
            split_axis=0,
            concat_axis=0,
            tiled=True,
        ),
        lax.all_to_all(
            to_slots(cache_live, cache_send, owner_count, per_pair),
            "dp",
            split_axis=0,
            concat_axis=0,
            tiled=True,
        ),
    )
    inverse = jnp.sum(
        group_index[:, None] * (cache_group[:, None] == group_index[None, :]).astype(jnp.int32),
        axis=0,
    )
    cache_slot = (my_rank - cache_offset[inverse]) % owner_count * per_pair + inverse // owner_count
    own_cache = got_cache.reshape((owner_count * per_pair,) + cache_grouped.shape[1:])[cache_slot]
    own_flags = got_flags.reshape(owner_count * per_pair)[cache_slot]
    own_cache = jnp.where(
        own_flags[:, None, None, None, None] > 0, own_cache, jnp.zeros_like(own_cache)
    )
    sequence = jnp.concatenate([own_cache, own_rows], axis=2)
    sequence = sequence.reshape((groups * pair_rows,) + sequence.shape[2:])
    live_rows = (jnp.arange(pair_rows, dtype=jnp.int32)[None, :] < own_counts[:, None]).reshape(
        groups * pair_rows
    )
    channels = spatial_weight.shape[1]
    weight_cut = temporal_weight
    conv_time = temporal_conv(
        lax.all_gather(sequence, "mp", axis=3, tiled=True), weight_cut, span_steps
    )
    square_sum = lax.psum(jnp.sum(conv_time * conv_time, axis=3), "mp")
    scaled = (
        conv_time
        * lax.rsqrt(square_sum / channels + 1e-06)[..., None]
        * norm_gain.astype(jnp.float32)
    )
    activated = jax.nn.silu(scaled).astype(jnp.bfloat16)
    weight_cut = spatial_weight
    conv_space = spatial_conv(lax.all_gather(activated, "mp", axis=3, tiled=True), weight_cut)
    latents = jnp.where(live_rows[:, None, None, None], conv_time + conv_space, 0.0).astype(
        jnp.bfloat16
    )
    return latents


CORES = 2
VMEM_LIMIT = 56 * 1024 * 1024


def shift_order(size):
    far = sorted(range(1, size), key=lambda k: (abs(k - size // 2), k))
    return [0] + far


def lane_iota(shape):
    return lax.broadcasted_iota(jnp.int32, shape, len(shape) - 1)


def pick(index, table):
    out = jnp.zeros_like(index)
    for at, value in enumerate(table):
        out = jnp.where(index == at, value, out)
    return out


def position_of(shift, order):
    out = jnp.int32(0)
    for at, k in enumerate(order):
        out = jnp.where(shift == k, jnp.int32(at), out)
    return out


def pack_kernel(order, pair_rows, mark_dead, offset_ref, flag_ref, own_ref, other_ref, *rest):
    outs, joined = rest[:-1], rest[-1]
    core = lax.axis_index("mp") % CORES
    tokens, _, part, rows = joined.shape
    joined[:, core] = own_ref[...].reshape(tokens, part, rows)
    joined[:, 1 - core] = other_ref[...].reshape(tokens, part, rows)
    shifts = len(order)
    groups = rows // pair_rows
    half_levels = groups // shifts // CORES
    slots = half_levels * pair_rows
    total = shifts * slots
    row = lane_iota((1, rows))
    place = pick(row // pair_rows % shifts, [position_of(offset_ref[j], order) for j in range(shifts)])
    level = row // (pair_rows * shifts) - core * half_levels
    target = place * slots + level * pair_rows + row % pair_rows
    target = jnp.where((level >= 0) & (level < half_levels), target, -1)
    hit = lax.broadcasted_iota(jnp.int32, (total, rows), 0) == target
    spread = (
        lax.broadcasted_iota(jnp.int32, (groups, rows), 0) == lane_iota((groups, rows)) // pair_rows
    ).astype(jnp.float32)
    flag = jnp.dot(flag_ref[...].astype(jnp.float32), spread, preferred_element_type=jnp.float32)
    if mark_dead:
        live = (row % pair_rows).astype(jnp.float32) < flag
        dead = jnp.sum(jnp.where(hit & jnp.logical_not(live), 1.0, 0.0), axis=1, keepdims=True) > 0.5
    else:
        hit = hit & (flag > 0.5)
    onehot = jnp.where(hit, 1.0, 0.0).astype(jnp.bfloat16)
    flat = joined.reshape(tokens * CORES * part, rows)
    step = 512
    for start in range(0, tokens * CORES * part, step):
        tile = lax.dot_general(
            onehot,
            flat[start : start + step],
            (((1,), (1,)), ((), ())),
            preferred_element_type=jnp.float32,
        )
        if mark_dead:
            tile = jnp.where(dead, jnp.inf, tile)
        tile = tile.astype(jnp.bfloat16)
        for at, out in enumerate(outs):
            out[:, start : start + step] = tile[at * slots : (at + 1) * slots]


def pack(order, pair_rows, mark_dead, offset, flag, own, other):
    rows = own.shape[1]
    shifts = len(order)
    slots = rows // shifts // CORES
    part = 64
    tokens = own.shape[0] // part
    width = own.shape[0] * CORES
    vmem = pl.BlockSpec(memory_space=pltpu.VMEM)
    return pl.pallas_call(
        functools.partial(pack_kernel, order, pair_rows, mark_dead),
        out_shape=[jax.ShapeDtypeStruct((slots, width), jnp.bfloat16)] * shifts,
        in_specs=[pl.BlockSpec(memory_space=pltpu.SMEM), vmem, vmem, vmem],
        out_specs=[vmem] * shifts,
        scratch_shapes=[pltpu.VMEM((tokens, CORES, part, rows), jnp.bfloat16)],
        compiler_params=pltpu.CompilerParams(vmem_limit_bytes=VMEM_LIMIT),
        cost_estimate=pl.CostEstimate(
            flops=2 * shifts * slots * width * rows, bytes_accessed=3 * width * rows, transcendentals=0
        ),
        name="pack_dead" if mark_dead else "pack_carried",
    )(offset, flag, own, other)


def choose_kernel(
    order, pair_rows, group_offset_ref, cache_offset_ref, group_ref, own0, own1, other0, other1, out
):
    core = lax.axis_index("mp") % CORES
    shifts = len(order)
    half, width = own0.shape
    groups = group_ref.shape[1]
    rows = groups * pair_rows
    half_levels = groups // shifts // CORES
    slots = half_levels * pair_rows
    column = lane_iota((1, rows))
    home = jnp.where(column < half, core, 1 - core)
    within = column % half
    shift_at = within // slots
    residue = jnp.zeros_like(column)
    for j in range(shifts):
        residue = jnp.where(shift_at == position_of(cache_offset_ref[j], order), j, residue)
    level = within % slots // pair_rows + home * half_levels
    cached = level * shifts + residue
    pickers = (lax.broadcasted_iota(jnp.int32, (groups, rows), 0) == cached).astype(jnp.float32)
    group = jnp.dot(
        group_ref[...].astype(jnp.float32), pickers, preferred_element_type=jnp.float32
    )
    group = (group + 0.5).astype(jnp.int32)
    place = pick(group % shifts, [position_of(group_offset_ref[j], order) for j in range(shifts)])
    goal = group // shifts - core * half_levels
    target = place * slots + goal * pair_rows + column % pair_rows
    target = jnp.where((goal >= 0) & (goal < half_levels), target, -1)
    onehot = jnp.where(
        lax.broadcasted_iota(jnp.int32, (half, rows), 0) == target, 1.0, 0.0
    ).astype(jnp.bfloat16)
    step = 512
    for side, (own, other) in enumerate(((own0, other0), (own1, other1))):
        for start in range(0, width, step):
            both = jnp.concatenate(
                [own[:, start : start + step], other[:, start : start + step]], axis=0
            )
            out[:, side * width + start : side * width + start + step] = jnp.dot(
                onehot, both, preferred_element_type=jnp.float32
            ).astype(jnp.bfloat16)


def choose(order, pair_rows, group_offset, cache_offset, group, own, other):
    half, width = own[0].shape
    vmem = pl.BlockSpec(memory_space=pltpu.VMEM)
    smem = pl.BlockSpec(memory_space=pltpu.SMEM)
    return pl.pallas_call(
        functools.partial(choose_kernel, order, pair_rows),
        out_shape=jax.ShapeDtypeStruct((half, 2 * width), jnp.bfloat16),
        in_specs=[smem, smem] + [vmem] * 5,
        out_specs=vmem,
        compiler_params=pltpu.CompilerParams(vmem_limit_bytes=VMEM_LIMIT),
        cost_estimate=pl.CostEstimate(
            flops=8 * half * half * width, bytes_accessed=12 * half * width, transcendentals=0
        ),
        name="choose_carried",
    )(group_offset, cache_offset, group, *own, *other)


def weights_kernel(taps, near, near_core, far_core, space, space_core, time_out, space_out, gain_out):
    index = lax.axis_index("mp")
    part = near.shape[1]
    inner = (near.shape[0] - 16) // taps
    side = inner // 2
    chip = index // CORES
    for tap in range(taps):
        for at in range(2):
            source = pl.ds(pl.multiple_of(tap * inner + (chip ^ at) * side, side), side)
            rows = slice(tap * inner + at * side, tap * inner + (at + 1) * side)
            for block, ref in enumerate((near, near_core)):
                time_out[rows, block * part : (block + 1) * part] = ref[source, :]
            for block in range(2):
                base = block * near.shape[0]
                source = pl.ds(
                    pl.multiple_of(base + tap * inner + (chip ^ at) * side, 16), side
                )
                time_out[rows, (2 + block) * part : (3 + block) * part] = far_core[source, :]
    gain_row = taps * inner
    gains = [near, near_core]
    for block, ref in enumerate(gains):
        gain_out[:, block * part : (block + 1) * part] = ref[gain_row : gain_row + 16, :]
    for block in range(2):
        base = block * near.shape[0] + gain_row
        gain_out[:, (2 + block) * part : (3 + block) * part] = far_core[base : base + 16, :]
    channels = 4 * part
    for tap in range(space.shape[0] // channels):
        for block in range(4):
            source = pl.ds(
                pl.multiple_of(tap * channels + (index ^ block) * part, part), part
            )
            rows = slice(tap * channels + block * part, tap * channels + (block + 1) * part)
            space_out[rows, :part] = space[source, :]
            space_out[rows, part:] = space_core[source, :]


def arrange_weights(taps, near, near_core, far_core, space, space_core):
    part = near.shape[1]
    vmem = pl.BlockSpec(memory_space=pltpu.VMEM)
    return pl.pallas_call(
        functools.partial(weights_kernel, taps),
        out_shape=[
            jax.ShapeDtypeStruct((near.shape[0] - 16, 4 * part), jnp.bfloat16),
            jax.ShapeDtypeStruct((space.shape[0], 2 * part), jnp.bfloat16),
            jax.ShapeDtypeStruct((16, 4 * part), jnp.bfloat16),
        ],
        in_specs=[vmem] * 5,
        out_specs=[vmem] * 3,
        compiler_params=pltpu.CompilerParams(vmem_limit_bytes=VMEM_LIMIT),
        cost_estimate=pl.CostEstimate(
            flops=0, bytes_accessed=4 * (near.size * 4 + space.size * 2), transcendentals=0
        ),
        name="arrange_weights",
    )(near, near_core, far_core, space, space_core)


def encode_kernel(count, width, *refs):
    near, far = refs[:count], refs[count : 2 * count]
    carried, time_w, space_w, gain_ref, kept, sent, seq, act = refs[2 * count :]
    slots = near[0].shape[0]
    rows = count * slots
    side = seq.shape[2] // 2
    channels = time_w.shape[1]
    half_width = carried.shape[1] // 2
    past = half_width // (side * width)
    span = near[0].shape[1] // (side * width)
    taps = time_w.shape[0] // (2 * side)
    tokens = width * rows
    for step in range(past):
        for w in range(width):
            lane = (step * width + w) * side
            at = slice(w * rows, (w + 1) * rows)
            seq[step, at, :side] = carried[:, lane : lane + side]
            seq[step, at, side:] = carried[:, half_width + lane : half_width + lane + side]
    for step in range(span):
        for w in range(width):
            lane = (step * width + w) * side
            for u in range(count):
                at = slice(w * rows + u * slots, w * rows + (u + 1) * slots)
                seq[past + step, at, :side] = near[u][:, lane : lane + side]
                seq[past + step, at, side:] = far[u][:, lane : lane + side]
    first = jnp.concatenate([ref[:, :side].astype(jnp.float32)[:, :1] for ref in near], axis=0)
    live = (first < jnp.inf)[None]
    gain = gain_ref[0:1, :].astype(jnp.float32)
    act[0:rows] = jnp.zeros((rows, channels), jnp.bfloat16)
    act[(width + 1) * rows :] = jnp.zeros((rows, channels), jnp.bfloat16)
    block = slots * width
    row_index = lax.broadcasted_iota(jnp.int32, (block, block), 0)
    column_index = lax.broadcasted_iota(jnp.int32, (block, block), 1)
    turn = jnp.where(
        (row_index // width == column_index % slots) & (row_index % width == column_index // slots),
        1.0,
        0.0,
    ).astype(jnp.bfloat16)
    for t in range(span):
        conv = jnp.dot(
            jnp.concatenate([seq[past + t - tap] for tap in range(taps)], axis=1),
            time_w[...],
            preferred_element_type=jnp.float32,
        )
        square = jnp.sum(conv * conv, axis=1, keepdims=True)
        scaled = conv * lax.rsqrt(square / channels + 1e-06) * gain
        act[rows : (width + 1) * rows] = jax.nn.silu(scaled).astype(jnp.bfloat16)
        kept_columns = space_w.shape[1]
        total = conv[:, :kept_columns] + jnp.dot(
            jnp.concatenate([act[tap * rows : tap * rows + tokens] for tap in range(3)], axis=1),
            space_w[...],
            preferred_element_type=jnp.float32,
        )
        total = jnp.where(live, total.reshape(width, rows, kept_columns), 0.0).astype(jnp.bfloat16)
        for u in range(count):
            part = total[:, u * slots : (u + 1) * slots].reshape(block, kept_columns)
            part = jnp.dot(turn, part, preferred_element_type=jnp.float32).astype(jnp.bfloat16)
            part = part.reshape(slots, width, kept_columns)
            at = slice(u * slots, (u + 1) * slots)
            kept[at, t] = part[:, :, : kept_columns // 2]
            sent[at, t] = part[:, :, kept_columns // 2 :]


def encode(width, span, index, near, far, carried, time_w, space_w, gain):
    count = len(near)
    slots, lanes = near[0].shape
    rows = count * slots
    side = lanes // (span * width)
    past = carried.shape[1] // 2 // (side * width)
    channels = time_w.shape[1]
    vmem = pl.BlockSpec(memory_space=pltpu.VMEM)
    part = space_w.shape[1] // 2
    out = jax.ShapeDtypeStruct((rows, span, width, part), jnp.bfloat16)
    tokens = rows * span * width
    return pl.pallas_call(
        functools.partial(encode_kernel, count, width),
        out_shape=[out, out],
        grid=(1,),
        in_specs=[vmem] * (2 * count)
        + [pl.BlockSpec((rows, carried.shape[1]), lambda i: (index, 0))]
        + [vmem] * 3,
        out_specs=[vmem] * 2,
        scratch_shapes=[
            pltpu.VMEM((past + span, width * rows, 2 * side), jnp.bfloat16),
            pltpu.VMEM(((width + 2) * rows, channels), jnp.bfloat16),
        ],
        compiler_params=pltpu.CompilerParams(vmem_limit_bytes=VMEM_LIMIT),
        cost_estimate=pl.CostEstimate(
            flops=2 * tokens * (time_w.size + space_w.size),
            bytes_accessed=2 * (time_w.size + space_w.size) + 16 * rows * lanes,
            transcendentals=tokens * channels,
        ),
        name="encode_rows",
    )(*near, *far, carried, time_w, space_w, gain)


def place_kernel(order, chunks, offset_ref, *refs):
    blocks, out = refs[:-1], refs[-1]
    core = lax.axis_index("mp") % CORES
    shifts = len(order)
    for chunk in range(len(chunks)):
        for u, shift in enumerate(chunks[chunk]):
            residue = jnp.int32(0)
            for j in range(shifts):
                residue = jnp.where(offset_ref[j] == shift, jnp.int32(j), residue)
            for kind in range(2):
                out[core ^ kind, :, residue] = blocks[kind * len(chunks) + chunk][u]


def place(order, chunks, pair_rows, offset, kept, got):
    count = len(chunks[0])
    rows, span, width, part = kept[0].shape
    half_levels = rows // count // pair_rows
    tail = (pair_rows, span, width, part)
    blocks = [a.reshape((count, half_levels) + tail) for a in kept + got]
    vmem = pl.BlockSpec(memory_space=pltpu.VMEM)
    out = pl.pallas_call(
        functools.partial(place_kernel, order, chunks),
        out_shape=jax.ShapeDtypeStruct((CORES, half_levels, len(order)) + tail, jnp.bfloat16),
        in_specs=[pl.BlockSpec(memory_space=pltpu.SMEM)] + [vmem] * len(blocks),
        out_specs=vmem,
        compiler_params=pltpu.CompilerParams(vmem_limit_bytes=VMEM_LIMIT),
        cost_estimate=pl.CostEstimate(
            flops=0, bytes_accessed=4 * sum(a.size for a in blocks), transcendentals=0
        ),
        name="place_rows",
    )(offset, *blocks)
    return out.reshape((-1, span, width, part))


def routed_local(
    frames,
    cache,
    group_offset,
    cache_offset,
    cache_group,
    group_rows,
    cache_live,
    temporal_weight,
    spatial_weight,
    norm_gain,
):
    shifts = lax.axis_size("dp")
    parts = lax.axis_size("mp")
    groups = group_offset.shape[0]
    rows, span, width, part_in = frames.shape
    pair_rows = rows // groups
    taps = temporal_weight.shape[0]
    order = shift_order(shifts)
    per_chunk = 2
    chunks = [order[i : i + per_chunk] for i in range(0, shifts, per_chunk)]

    def flip(x, mask):
        return lax.ppermute(x, "mp", [(i, i ^ mask) for i in range(parts)])

    def send(x, shift):
        if shift == 0:
            return x
        return lax.ppermute(x, "dp", [(i, (i + shift) % shifts) for i in range(shifts)])

    cache_rows = cache.transpose((1, 2, 3, 0)).reshape((-1, rows))
    frame_rows = frames.transpose((1, 2, 3, 0)).reshape((-1, rows))
    cache_packed = pack(
        order,
        pair_rows,
        False,
        cache_offset,
        cache_live.reshape((1, groups)),
        cache_rows,
        flip(cache_rows, 1),
    )
    frame_packed = pack(
        order,
        pair_rows,
        True,
        group_offset,
        group_rows.reshape((1, groups)),
        frame_rows,
        flip(frame_rows, 1),
    )
    flat_time = temporal_weight.reshape((-1, temporal_weight.shape[2]))
    near = jnp.concatenate([flat_time, jnp.broadcast_to(norm_gain[None], (16, norm_gain.shape[0]))], axis=0)
    space = spatial_weight.reshape((-1, spatial_weight.shape[2]))
    far = flip(near, 2)
    near_core, far_core, space_core = flip(near, 1), flip(far, 1), flip(space, 1)
    time_w, space_w, gain = arrange_weights(
        taps, near, near_core, jnp.concatenate([far, far_core], axis=0), space, space_core
    )
    cache_near = [send(x, k) for x, k in zip(cache_packed, order)]
    cache_far = [flip(x, 2) for x in cache_near]
    own = jnp.concatenate(cache_near, axis=0), jnp.concatenate(cache_far, axis=0)
    other = flip(own[0], 1), flip(own[1], 1)
    carried = choose(
        order, pair_rows, group_offset, cache_offset, cache_group.reshape((1, groups)), own, other
    )
    frame_near = [send(x, k) for x, k in zip(frame_packed, order)]
    frame_far = [flip(x, 2) for x in frame_near]
    kept, got = [], []
    for index in range(len(chunks)):
        at = slice(index * per_chunk, (index + 1) * per_chunk)
        keep, give = encode(
            width, span, index, frame_near[at], frame_far[at], carried, time_w, space_w, gain
        )
        kept.append(keep)
        got.append(flip(give, 1))
    return place(order, chunks, pair_rows, group_offset, kept, got)


def fits(mesh, frames, group_offset, temporal_weight):
    shifts, parts = mesh.shape["dp"], mesh.shape["mp"]
    groups = group_offset.shape[0]
    rows = frames.shape[0] // shifts
    if parts != 4 or frames.shape[3] != 64 * parts or groups > 256:
        return False
    if temporal_weight.shape[2] != 128 * parts or shifts % 2:
        return False
    if groups % (shifts * CORES):
        return False
    return rows // shifts // CORES % 16 == 0 and rows % 128 == 0


def solution(mesh):
    in_specs = (
        P("dp", None, None, "mp"),
        P("dp", None, None, "mp"),
        P(),
        P(),
        P(),
        P("dp", None),
        P("dp"),
        P(None, None, "mp"),
        P(None, None, "mp"),
        P("mp"),
    )
    out_specs = P("dp", None, None, "mp")

    def call(*args):
        body = routed_local if fits(mesh, args[0], args[2], args[7]) else plain_local
        return jax.shard_map(
            body, mesh=mesh, in_specs=in_specs, out_specs=out_specs, check_vma=False
        )(*args)

    return call
```

```python
import functools

import jax
import jax.numpy as jnp
from jax import lax
from jax.experimental import pallas as pl
from jax.experimental.pallas import tpu as pltpu
from jax.sharding import PartitionSpec as P


def temporal_conv(sequence, weight_part, span_steps):
    taps = weight_part.shape[0]
    windows = [
        sequence[:, taps - 1 - tap_index : taps - 1 - tap_index + span_steps]
        for tap_index in range(taps)
    ]
    joined = jnp.concatenate(windows, axis=3)
    flat_weight = weight_part.reshape((taps * weight_part.shape[1], weight_part.shape[2]))
    return jnp.einsum("rtwc,cd->rtwd", joined, flat_weight, preferred_element_type=jnp.float32)


def spatial_conv(activated, weight_part):
    width = activated.shape[2]
    padded = jnp.pad(activated, ((0, 0), (0, 0), (1, 1), (0, 0)))
    joined = jnp.concatenate(
        [padded[:, :, tap_index : tap_index + width] for tap_index in range(3)], axis=3
    )
    flat_weight = weight_part.reshape((3 * weight_part.shape[1], weight_part.shape[2]))
    return jnp.einsum("rtwc,cd->rtwd", joined, flat_weight, preferred_element_type=jnp.float32)


def to_slots(values, slot_index, owner_count, per_pair):
    buffer = (
        jnp.zeros((owner_count * per_pair,) + values.shape[1:], values.dtype)
        .at[slot_index]
        .set(values)
    )
    return buffer.reshape((owner_count, per_pair) + values.shape[1:])


def plain_local(
    frames,
    cache,
    group_offset,
    cache_offset,
    cache_group,
    group_rows,
    cache_live,
    temporal_weight,
    spatial_weight,
    norm_gain,
):
    owner_count = lax.axis_size("dp")
    my_rank = lax.axis_index("dp")
    groups = group_offset.shape[0]
    pair_rows = frames.shape[0] // groups
    span_steps = frames.shape[1]
    per_pair = (groups + owner_count - 1) // owner_count
    group_index = jnp.arange(groups, dtype=jnp.int32)
    slot_level = group_index // owner_count
    grouped = frames.reshape((groups, pair_rows) + frames.shape[1:])
    counts = group_rows.reshape(groups)
    send_slot = (my_rank + group_offset) % owner_count * per_pair + slot_level
    got_rows, got_counts = (
        lax.all_to_all(
            to_slots(grouped, send_slot, owner_count, per_pair),
            "dp",
            split_axis=0,
            concat_axis=0,
            tiled=True,
        ),
        lax.all_to_all(
            to_slots(counts, send_slot, owner_count, per_pair),
            "dp",
            split_axis=0,
            concat_axis=0,
            tiled=True,
        ),
    )
    take_slot = (my_rank - group_offset) % owner_count * per_pair + slot_level
    own_rows = got_rows.reshape((owner_count * per_pair,) + grouped.shape[1:])[take_slot]
    own_counts = got_counts.reshape(owner_count * per_pair)[take_slot]
    cache_grouped = cache.reshape((groups, pair_rows) + cache.shape[1:])
    cache_send = (my_rank + cache_offset) % owner_count * per_pair + slot_level
    got_cache, got_flags = (
        lax.all_to_all(
            to_slots(cache_grouped, cache_send, owner_count, per_pair),
            "dp",
            split_axis=0,
            concat_axis=0,
            tiled=True,
        ),
        lax.all_to_all(
            to_slots(cache_live, cache_send, owner_count, per_pair),
            "dp",
            split_axis=0,
            concat_axis=0,
            tiled=True,
        ),
    )
    inverse = jnp.sum(
        group_index[:, None] * (cache_group[:, None] == group_index[None, :]).astype(jnp.int32),
        axis=0,
    )
    cache_slot = (my_rank - cache_offset[inverse]) % owner_count * per_pair + inverse // owner_count
    own_cache = got_cache.reshape((owner_count * per_pair,) + cache_grouped.shape[1:])[cache_slot]
    own_flags = got_flags.reshape(owner_count * per_pair)[cache_slot]
    own_cache = jnp.where(
        own_flags[:, None, None, None, None] > 0, own_cache, jnp.zeros_like(own_cache)
    )
    sequence = jnp.concatenate([own_cache, own_rows], axis=2)
    sequence = sequence.reshape((groups * pair_rows,) + sequence.shape[2:])
    live_rows = (jnp.arange(pair_rows, dtype=jnp.int32)[None, :] < own_counts[:, None]).reshape(
        groups * pair_rows
    )
    channels = spatial_weight.shape[1]
    weight_cut = temporal_weight
    conv_time = temporal_conv(
        lax.all_gather(sequence, "mp", axis=3, tiled=True), weight_cut, span_steps
    )
    square_sum = lax.psum(jnp.sum(conv_time * conv_time, axis=3), "mp")
    scaled = (
        conv_time
        * lax.rsqrt(square_sum / channels + 1e-06)[..., None]
        * norm_gain.astype(jnp.float32)
    )
    activated = jax.nn.silu(scaled).astype(jnp.bfloat16)
    weight_cut = spatial_weight
    conv_space = spatial_conv(lax.all_gather(activated, "mp", axis=3, tiled=True), weight_cut)
    latents = jnp.where(live_rows[:, None, None, None], conv_time + conv_space, 0.0).astype(
        jnp.bfloat16
    )
    return latents


CORES = 2
MIB = 1024 * 1024
Z_DEPTH = 4
Y_DEPTH = 2
C_CUTS = ((0, 4), (4, 8))
F_CUTS = ((0, 4), (4, 6), (6, 8))
CHOSEN = 6


def shift_order(size):
    far = sorted(range(1, size), key=lambda k: (abs(k - size // 2), k))
    return [0] + far


def lane_iota(shape):
    return lax.broadcasted_iota(jnp.int32, shape, len(shape) - 1)


def pick(index, table):
    out = jnp.zeros_like(index)
    for at, value in enumerate(table):
        out = jnp.where(index == at, value, out)
    return out


def position_of(shift, order):
    out = jnp.int32(0)
    for at, k in enumerate(order):
        out = jnp.where(shift == k, jnp.int32(at), out)
    return out


def pack_kernel(order, pair_rows, mark_dead, offset_ref, flag_ref, *refs):
    shifts = len(order)
    outs = refs[-shifts - (1 if mark_dead else 0) :][:shifts]
    groups = flag_ref.shape[1]
    rows = groups * pair_rows
    levels = groups // shifts
    first = 0
    if mark_dead:
        own_ref, other_ref, joined = refs[0], refs[1], refs[-1]
        tokens, _, part, _ = joined.shape
        joined[:, 0] = own_ref[...].reshape(tokens, part, rows)
        joined[:, 1] = other_ref[...].reshape(tokens, part, rows)
        flat = joined.reshape(tokens * CORES * part, rows)
        levels = levels // CORES
        first = lax.axis_index("mp") % CORES * levels
    else:
        flat = refs[0]
    slots = levels * pair_rows
    total = shifts * slots
    row = lane_iota((1, rows))
    place = pick(row // pair_rows % shifts, [position_of(offset_ref[j], order) for j in range(shifts)])
    level = row // (pair_rows * shifts) - first
    target = place * slots + level * pair_rows + row % pair_rows
    target = jnp.where((level >= 0) & (level < levels), target, -1)
    hit = lax.broadcasted_iota(jnp.int32, (total, rows), 0) == target
    spread = (
        lax.broadcasted_iota(jnp.int32, (groups, rows), 0) == lane_iota((groups, rows)) // pair_rows
    ).astype(jnp.float32)
    flag = jnp.dot(flag_ref[...].astype(jnp.float32), spread, preferred_element_type=jnp.float32)
    if mark_dead:
        live = (row % pair_rows).astype(jnp.float32) < flag
        dead = jnp.sum(jnp.where(hit & jnp.logical_not(live), 1.0, 0.0), axis=1, keepdims=True) > 0.5
    else:
        hit = hit & (flag > 0.5)
    onehot = jnp.where(hit, 1.0, 0.0).astype(jnp.bfloat16)
    step = 512
    for start in range(0, flat.shape[0], step):
        tile = lax.dot_general(
            onehot,
            flat[start : start + step],
            (((1,), (1,)), ((), ())),
            preferred_element_type=jnp.float32,
        )
        if mark_dead:
            tile = jnp.where(dead, jnp.inf, tile)
        tile = tile.astype(jnp.bfloat16)
        for at, out in enumerate(outs):
            out[:, start : start + step] = tile[at * slots : (at + 1) * slots]


def pack(order, pair_rows, mark_dead, offset, flag, *sources):
    height, rows = sources[0].shape
    shifts = len(order)
    slots = rows // shifts // len(sources)
    width = height * len(sources)
    vmem = pl.BlockSpec(memory_space=pltpu.VMEM)
    scratch = []
    if mark_dead:
        part = 64
        scratch = [pltpu.VMEM((height // part, CORES, part, rows), jnp.bfloat16)]
    return pl.pallas_call(
        functools.partial(pack_kernel, order, pair_rows, mark_dead),
        out_shape=[jax.ShapeDtypeStruct((slots, width), jnp.bfloat16)] * shifts,
        in_specs=[pl.BlockSpec(memory_space=pltpu.SMEM)] + [vmem] * (1 + len(sources)),
        out_specs=[vmem] * shifts,
        scratch_shapes=scratch,
        compiler_params=pltpu.CompilerParams(vmem_limit_bytes=16 * MIB),
        cost_estimate=pl.CostEstimate(
            flops=2 * shifts * slots * width * rows, bytes_accessed=2 * width * rows, transcendentals=0
        ),
        name="pack_dead" if mark_dead else "pack_carried",
    )(offset, flag, *sources)


def choose_kernel(order, pair_rows, count, group_offset_ref, cache_offset_ref, group_ref, *refs):
    shifts = len(order)
    near, far, near_other, far_other = (refs[i * count : (i + 1) * count] for i in range(4))
    outs = refs[4 * count :]
    core = lax.axis_index("mp") % CORES
    groups = group_ref.shape[1]
    rows = groups * pair_rows
    width = near[0].shape[1]
    slots = rows // shifts
    half_levels = groups // shifts // CORES
    column = lane_iota((1, rows))
    shift_at = column // slots
    residue = jnp.zeros_like(column)
    for j in range(shifts):
        residue = jnp.where(shift_at == position_of(cache_offset_ref[j], order), j, residue)
    cached = column % slots // pair_rows * shifts + residue
    pickers = (lax.broadcasted_iota(jnp.int32, (groups, rows), 0) == cached).astype(jnp.float32)
    group = jnp.dot(
        group_ref[...].astype(jnp.float32), pickers, preferred_element_type=jnp.float32
    )
    group = (group + 0.5).astype(jnp.int32)
    place = pick(group % shifts, [position_of(group_offset_ref[j], order) for j in range(shifts)])
    goal = group // shifts - core * half_levels
    half = rows // CORES
    target = (place * half_levels + goal) * pair_rows + column % pair_rows
    target = jnp.where((goal >= 0) & (goal < half_levels), target, -1)
    onehot = jnp.where(
        lax.broadcasted_iota(jnp.int32, (half, rows), 0) == target, 1.0, 0.0
    ).astype(jnp.bfloat16)
    step = 512
    part = 64
    piece = half // len(outs)
    for side, pair in enumerate(((near, near_other), (far, far_other))):
        for start in range(0, width, step):
            got = [
                jnp.dot(
                    onehot,
                    jnp.concatenate([ref[:, start : start + step] for ref in one], axis=0),
                    preferred_element_type=jnp.float32,
                )
                for one in pair
            ]
            mixed = jnp.concatenate(
                [one[:, at : at + part] for at in range(0, step, part) for one in got], axis=1
            ).astype(jnp.bfloat16)
            for at, out in enumerate(outs):
                lane = CORES * (side * width + start)
                out[:, lane : lane + CORES * step] = mixed[at * piece : (at + 1) * piece]


def choose(order, pair_rows, pieces, group_offset, cache_offset, group, *sources):
    width = sources[0][0].shape[1]
    rows = group.shape[1] * pair_rows
    vmem = pl.BlockSpec(memory_space=pltpu.VMEM)
    smem = pl.BlockSpec(memory_space=pltpu.SMEM)
    flat = [x for source in sources for x in source]
    out = jax.ShapeDtypeStruct((rows // CORES // pieces, 2 * CORES * width), jnp.bfloat16)
    return pl.pallas_call(
        functools.partial(choose_kernel, order, pair_rows, len(sources[0])),
        out_shape=[out] * pieces,
        in_specs=[smem, smem] + [vmem] * (1 + len(flat)),
        out_specs=[vmem] * pieces,
        compiler_params=pltpu.CompilerParams(vmem_limit_bytes=16 * MIB),
        cost_estimate=pl.CostEstimate(
            flops=4 * rows * rows * width, bytes_accessed=12 * rows * width, transcendentals=0
        ),
        name="choose_carried",
    )(group_offset, cache_offset, group, *flat)


def weights_kernel(taps, own, other, far, time_out, space_out, gain_out):
    index = lax.axis_index("mp")
    part = own.shape[1]
    height = far.shape[0] // 2
    inner = (height - 16) // taps
    side = inner // 4
    sources = ((own, 0), (other, 0), (far, 0), (far, height))
    for block, (ref, base) in enumerate(sources):
        columns = slice(block * part, (block + 1) * part)
        for tap in range(taps):
            for at in range(4):
                begin = pl.multiple_of(base + tap * inner + (index ^ at) * side, 16)
                rows = slice(tap * inner + at * side, tap * inner + (at + 1) * side)
                time_out[rows, columns] = ref[pl.ds(begin, side), :]
        gain_out[:, columns] = ref[base + taps * inner : base + height, :]
    channels = 4 * part
    for tap in range(3):
        for block in range(4):
            begin = pl.multiple_of(height + tap * channels + (index ^ block) * part, 16)
            rows = slice(tap * channels + block * part, tap * channels + (block + 1) * part)
            space_out[rows, :part] = own[pl.ds(begin, part), :]
            space_out[rows, part:] = other[pl.ds(begin, part), :]


def arrange_weights(taps, own, other, far):
    part = own.shape[1]
    height = far.shape[0] // 2
    vmem = pl.BlockSpec(memory_space=pltpu.VMEM)
    return pl.pallas_call(
        functools.partial(weights_kernel, taps),
        out_shape=[
            jax.ShapeDtypeStruct((height - 16, 4 * part), jnp.bfloat16),
            jax.ShapeDtypeStruct((own.shape[0] - height, 2 * part), jnp.bfloat16),
            jax.ShapeDtypeStruct((16, 4 * part), jnp.bfloat16),
        ],
        in_specs=[vmem] * 3,
        out_specs=[vmem] * 3,
        compiler_params=pltpu.CompilerParams(vmem_limit_bytes=12 * MIB),
        cost_estimate=pl.CostEstimate(
            flops=0, bytes_accessed=8 * own.size, transcendentals=0
        ),
        name="arrange_weights",
    )(own, other, far)


def encode_kernel(cuts, width, *refs):
    count = len(cuts[0]) + len(cuts[1])
    near, far = refs[: len(cuts[0])], refs[len(cuts[0]) : count]
    carried, time_w, space_w, gain_ref, kept, sent, seq, act, rest = refs[count:]
    rows = carried.shape[0]
    channels = time_w.shape[1]
    span = seq.shape[0]
    tokens = width * rows
    inner = near[0].shape[1] // (span * width) * 2
    side = inner // 2
    taps = time_w.shape[0] // inner
    half_width = carried.shape[1] // 2
    past = half_width // (side * width)

    def fill(step, rows_at, column, value):
        for t in range(span):
            tap = past + t - step
            if 0 <= tap < taps:
                seq[t, rows_at, tap * inner + column : tap * inner + column + side] = value

    for w in range(width):
        for step in range(past):
            lane = (step * width + w) * side
            for column, base in ((0, 0), (side, half_width)):
                value = carried[:, base + lane : base + lane + side]
                fill(step, slice(w * rows, (w + 1) * rows), column, value)
        for step in range(span):
            lane = (step * width + w) * side
            for column, sources, cut in ((0, near, cuts[0]), (side, far, cuts[1])):
                begin = w * rows
                for ref, (low, high) in zip(sources, cut):
                    value = ref[low:high, lane : lane + side]
                    fill(past + step, slice(begin, begin + high - low), column, value)
                    begin += high - low
    first = jnp.concatenate(
        [ref[a:b, :side].astype(jnp.float32)[:, :1] for ref, (a, b) in zip(near, cuts[0])], axis=0
    )
    live = (first < jnp.inf)[None]
    gain = gain_ref[0:1, :].astype(jnp.float32)
    kept_columns = space_w.shape[1]
    edge = jnp.zeros((rows, channels), jnp.bfloat16)
    for t in range(span):
        act[t, 0:rows, :channels] = edge
        act[t, tokens - rows :, 2 * channels :] = edge
    tile = 256
    for t in range(span):
        for start in range(0, tokens, tile):
            conv = jnp.dot(
                seq[t, start : start + tile], time_w[...], preferred_element_type=jnp.float32
            )
            square = jnp.sum(conv * conv, axis=1, keepdims=True)
            rest[t, start : start + tile] = conv[:, :kept_columns]
            scaled = conv * lax.rsqrt(square / channels + 1e-06) * gain
            value = jax.nn.silu(scaled).astype(jnp.bfloat16)
            act[t, start : start + tile, channels : 2 * channels] = value
            if start + tile < tokens:
                act[t, start + rows : start + rows + tile, :channels] = value
            else:
                act[t, start + rows : tokens, :channels] = value[: tile - rows]
            if start > 0:
                act[t, start - rows : start - rows + tile, 2 * channels :] = value
            else:
                act[t, : tile - rows, 2 * channels :] = value[rows:]
    tile = 256
    for t in range(span):
        for start in range(0, tokens, tile):
            total = rest[t, start : start + tile] + jnp.dot(
                act[t, start : start + tile], space_w[...], preferred_element_type=jnp.float32
            )
            wide = tile // rows
            total = jnp.where(live, total.reshape(wide, rows, kept_columns), 0.0)
            total = jnp.swapaxes(total, 0, 1).astype(jnp.bfloat16)
            place = slice(start // rows, start // rows + wide)
            kept[:, t, place] = total[:, :, : kept_columns // 2]
            sent[:, t, place] = total[:, :, kept_columns // 2 :]


def encode(width, span, near, far, carried, time_w, space_w, gain):
    cuts = [[(a, b) for _, a, b in pieces] for pieces in (near, far)]
    arrays = [x for pieces in (near, far) for x, _, _ in pieces]
    rows, lanes = carried.shape[0], arrays[0].shape[1]
    channels = time_w.shape[1]
    vmem = pl.BlockSpec(memory_space=pltpu.VMEM)
    part = space_w.shape[1] // 2
    out = jax.ShapeDtypeStruct((rows, span, width, part), jnp.bfloat16)
    tokens = rows * span * width
    return pl.pallas_call(
        functools.partial(encode_kernel, cuts, width),
        out_shape=[out, out],
        in_specs=[vmem] * (len(arrays) + 4),
        out_specs=[vmem] * 2,
        scratch_shapes=[
            pltpu.VMEM((span, width * rows, time_w.shape[0]), jnp.bfloat16),
            pltpu.VMEM((span, width * rows, space_w.shape[0]), jnp.bfloat16),
            pltpu.VMEM((span, width * rows, space_w.shape[1]), jnp.float32),
        ],
        compiler_params=pltpu.CompilerParams(vmem_limit_bytes=24 * MIB),
        cost_estimate=pl.CostEstimate(
            flops=2 * tokens * (time_w.size + space_w.size),
            bytes_accessed=2 * (time_w.size + space_w.size) + 16 * rows * lanes,
            transcendentals=tokens * channels,
        ),
        name="encode_rows",
    )(*arrays, carried, time_w, space_w, gain)


def place_kernel(order, chunks, offset_ref, *refs):
    blocks, out = refs[:-1], refs[-1]
    core = lax.axis_index("mp") % CORES
    shifts = len(order)
    for chunk in range(len(chunks)):
        for u, shift in enumerate(chunks[chunk]):
            residue = jnp.int32(0)
            for j in range(shifts):
                residue = jnp.where(offset_ref[j] == shift, jnp.int32(j), residue)
            for kind in range(2):
                out[core ^ kind, :, residue] = blocks[kind * len(chunks) + chunk][u]


def place(order, chunks, pair_rows, offset, kept, got):
    count = len(chunks[0])
    rows, span, width, part = kept[0].shape
    half_levels = rows // count // pair_rows
    tail = (pair_rows, span, width, part)
    blocks = [a.reshape((count, half_levels) + tail) for a in kept + got]
    vmem = pl.BlockSpec(memory_space=pltpu.VMEM)
    out = pl.pallas_call(
        functools.partial(place_kernel, order, chunks),
        out_shape=jax.ShapeDtypeStruct((CORES, half_levels, len(order)) + tail, jnp.bfloat16),
        in_specs=[pl.BlockSpec(memory_space=pltpu.SMEM)] + [vmem] * len(blocks),
        out_specs=vmem,
        compiler_params=pltpu.CompilerParams(vmem_limit_bytes=12 * MIB),
        cost_estimate=pl.CostEstimate(
            flops=0, bytes_accessed=4 * sum(a.size for a in blocks), transcendentals=0
        ),
        name="place_rows",
    )(offset, *blocks)
    return out.reshape((-1, span, width, part))


def routed_local(
    frames,
    cache,
    group_offset,
    cache_offset,
    cache_group,
    group_rows,
    cache_live,
    temporal_weight,
    spatial_weight,
    norm_gain,
):
    shifts = lax.axis_size("dp")
    parts = lax.axis_size("mp")
    groups = group_offset.shape[0]
    rows, span, width, part_in = frames.shape
    pair_rows = rows // groups
    taps = temporal_weight.shape[0]
    order = shift_order(shifts)
    per_chunk = 2
    chunks = [order[i : i + per_chunk] for i in range(0, shifts, per_chunk)]

    def after(x, *cells):
        got = lax.optimization_barrier((x, *[cell[0] for cell in cells]))
        for cell, value in zip(cells, got[1:]):
            cell[0] = value
        return got[0]

    lanes = {}

    def move(x, lane, depth, axis, pairs, cells=()):
        line = lanes.setdefault(lane, [])
        cells = list(cells) + (line[-depth : len(line) - depth + 1] if len(line) >= depth else [])
        if cells:
            x = after(x, *cells)
        line.append([lax.ppermute(x, axis, pairs)])
        return line[-1]

    def flip(x, mask, lane, depth, *cells):
        return move(x, lane, depth, "mp", [(i, i ^ mask) for i in range(parts)], cells)

    def send(x, shift, *cells):
        if shift == 0:
            return [x]
        return move(x, "z", Z_DEPTH, "dp", [(i, (i + shift) % shifts) for i in range(shifts)], cells)

    def join(pieces):
        if len(pieces) == 1:
            return pieces[0][0]
        return jnp.concatenate([x[0] for x in pieces], axis=0)

    cache_rows = cache.transpose((1, 2, 3, 0)).reshape((-1, rows))
    frame_rows = frames.transpose((1, 2, 3, 0)).reshape((-1, rows))
    frame_swapped = flip(frame_rows, 1, "core", 3)
    cache_packed = pack(
        order, pair_rows, False, cache_offset, cache_live.reshape((1, groups)), cache_rows
    )
    frame_packed = [
        [x]
        for x in pack(
            order,
            pair_rows,
            True,
            group_offset,
            group_rows.reshape((1, groups)),
            frame_rows,
            frame_swapped[0],
        )
    ]
    part = norm_gain.shape[0]
    time_rows = taps * temporal_weight.shape[1] + 16
    own_w = jnp.concatenate(
        [
            temporal_weight.reshape((-1, part)),
            jnp.broadcast_to(norm_gain[None], (16, part)),
            spatial_weight.reshape((-1, part)),
        ],
        axis=0,
    )
    other_w = flip(own_w, 1, "core", 3)
    far_w = flip(
        jnp.concatenate([own_w[:time_rows], other_w[0][:time_rows]], axis=0), 2, "y", 2
    )
    arranged = [[x] for x in arrange_weights(taps, own_w, other_w[0], far_w[0])]
    wait = {1: [frame_packed[0]], 2: [other_w], 5: [arranged[0]]}
    cache_near = [send(x, k, *wait.get(i, [])) for i, (x, k) in enumerate(zip(cache_packed, order))]
    near, far = [], []
    for a, b in C_CUTS:
        near.append([join(cache_near[a:b])])
        far.append(flip(near[-1][0], 2, "y", Y_DEPTH))
    near_other = [flip(x[0], 1, "core", 3) for x in near]
    far_other = [flip(x[0], 1, "core", 3) for x in far]
    carried = [
        [x]
        for x in choose(
            order,
            pair_rows,
            len(chunks),
            group_offset,
            cache_offset,
            cache_group.reshape((1, groups)),
            *[[x[0] for x in source] for source in (near, far, near_other, far_other)],
        )
    ]
    wait = {CHOSEN: [carried[0]]}
    frame_near = [
        send(x[0], k, *wait.get(i, [])) for i, (x, k) in enumerate(zip(frame_packed, order))
    ]

    def forward(pieces):
        return flip(join(pieces), 2, "y", Y_DEPTH)

    frame_far = {}
    for a, b in F_CUTS:
        cell = forward(frame_near[a:b])
        frame_far.update({at: (cell, at - a) for at in range(a, b)})
    slots = frame_near[0][0].shape[0]
    kept, got = [], []
    for index in range(len(chunks)):
        picked = range(index * per_chunk, (index + 1) * per_chunk)
        ours = [(frame_near[at][0], 0, slots) for at in picked]
        theirs = [
            (frame_far[at][0][0], frame_far[at][1] * slots, (frame_far[at][1] + 1) * slots)
            for at in picked
        ]
        keep, give = encode(
            width, span, ours, theirs, carried[index][0], *[x[0] for x in arranged]
        )
        kept.append(keep)
        got.append(flip(give, 1, "core", 3)[0])
    return place(order, chunks, pair_rows, group_offset, kept, got)


def fits(mesh, frames, group_offset, temporal_weight):
    shifts, parts = mesh.shape["dp"], mesh.shape["mp"]
    groups = group_offset.shape[0]
    rows = frames.shape[0] // shifts
    if parts != 4 or frames.shape[3] != 64 * parts or groups > 256:
        return False
    if temporal_weight.shape[2] != 128 * parts or shifts % 2:
        return False
    if groups % (shifts * CORES):
        return False
    return rows // shifts // CORES % 16 == 0 and rows % 128 == 0


def solution(mesh):
    in_specs = (
        P("dp", None, None, "mp"),
        P("dp", None, None, "mp"),
        P(),
        P(),
        P(),
        P("dp", None),
        P("dp"),
        P(None, None, "mp"),
        P(None, None, "mp"),
        P("mp"),
    )
    out_specs = P("dp", None, None, "mp")

    def call(*args):
        body = routed_local if fits(mesh, args[0], args[2], args[7]) else plain_local
        return jax.shard_map(
            body, mesh=mesh, in_specs=in_specs, out_specs=out_specs, check_vma=False
        )(*args)

    return call
```

```python
import functools

import jax
import jax.numpy as jnp
from jax import lax
from jax.experimental import pallas as pl
from jax.experimental.pallas import tpu as pltpu
from jax.sharding import PartitionSpec as P


def temporal_conv(sequence, weight_part, span_steps):
    taps = weight_part.shape[0]
    windows = [
        sequence[:, taps - 1 - tap_index : taps - 1 - tap_index + span_steps]
        for tap_index in range(taps)
    ]
    joined = jnp.concatenate(windows, axis=3)
    flat_weight = weight_part.reshape((taps * weight_part.shape[1], weight_part.shape[2]))
    return jnp.einsum("rtwc,cd->rtwd", joined, flat_weight, preferred_element_type=jnp.float32)


def spatial_conv(activated, weight_part):
    width = activated.shape[2]
    padded = jnp.pad(activated, ((0, 0), (0, 0), (1, 1), (0, 0)))
    joined = jnp.concatenate(
        [padded[:, :, tap_index : tap_index + width] for tap_index in range(3)], axis=3
    )
    flat_weight = weight_part.reshape((3 * weight_part.shape[1], weight_part.shape[2]))
    return jnp.einsum("rtwc,cd->rtwd", joined, flat_weight, preferred_element_type=jnp.float32)


def to_slots(values, slot_index, owner_count, per_pair):
    buffer = (
        jnp.zeros((owner_count * per_pair,) + values.shape[1:], values.dtype)
        .at[slot_index]
        .set(values)
    )
    return buffer.reshape((owner_count, per_pair) + values.shape[1:])


def plain_local(
    frames,
    cache,
    group_offset,
    cache_offset,
    cache_group,
    group_rows,
    cache_live,
    temporal_weight,
    spatial_weight,
    norm_gain,
):
    owner_count = lax.axis_size("dp")
    my_rank = lax.axis_index("dp")
    groups = group_offset.shape[0]
    pair_rows = frames.shape[0] // groups
    span_steps = frames.shape[1]
    per_pair = (groups + owner_count - 1) // owner_count
    group_index = jnp.arange(groups, dtype=jnp.int32)
    slot_level = group_index // owner_count
    grouped = frames.reshape((groups, pair_rows) + frames.shape[1:])
    counts = group_rows.reshape(groups)
    send_slot = (my_rank + group_offset) % owner_count * per_pair + slot_level
    got_rows, got_counts = (
        lax.all_to_all(
            to_slots(grouped, send_slot, owner_count, per_pair),
            "dp",
            split_axis=0,
            concat_axis=0,
            tiled=True,
        ),
        lax.all_to_all(
            to_slots(counts, send_slot, owner_count, per_pair),
            "dp",
            split_axis=0,
            concat_axis=0,
            tiled=True,
        ),
    )
    take_slot = (my_rank - group_offset) % owner_count * per_pair + slot_level
    own_rows = got_rows.reshape((owner_count * per_pair,) + grouped.shape[1:])[take_slot]
    own_counts = got_counts.reshape(owner_count * per_pair)[take_slot]
    cache_grouped = cache.reshape((groups, pair_rows) + cache.shape[1:])
    cache_send = (my_rank + cache_offset) % owner_count * per_pair + slot_level
    got_cache, got_flags = (
        lax.all_to_all(
            to_slots(cache_grouped, cache_send, owner_count, per_pair),
            "dp",
            split_axis=0,
            concat_axis=0,
            tiled=True,
        ),
        lax.all_to_all(
            to_slots(cache_live, cache_send, owner_count, per_pair),
            "dp",
            split_axis=0,
            concat_axis=0,
            tiled=True,
        ),
    )
    inverse = jnp.sum(
        group_index[:, None] * (cache_group[:, None] == group_index[None, :]).astype(jnp.int32),
        axis=0,
    )
    cache_slot = (my_rank - cache_offset[inverse]) % owner_count * per_pair + inverse // owner_count
    own_cache = got_cache.reshape((owner_count * per_pair,) + cache_grouped.shape[1:])[cache_slot]
    own_flags = got_flags.reshape(owner_count * per_pair)[cache_slot]
    own_cache = jnp.where(
        own_flags[:, None, None, None, None] > 0, own_cache, jnp.zeros_like(own_cache)
    )
    sequence = jnp.concatenate([own_cache, own_rows], axis=2)
    sequence = sequence.reshape((groups * pair_rows,) + sequence.shape[2:])
    live_rows = (jnp.arange(pair_rows, dtype=jnp.int32)[None, :] < own_counts[:, None]).reshape(
        groups * pair_rows
    )
    channels = spatial_weight.shape[1]
    weight_cut = temporal_weight
    conv_time = temporal_conv(
        lax.all_gather(sequence, "mp", axis=3, tiled=True), weight_cut, span_steps
    )
    square_sum = lax.psum(jnp.sum(conv_time * conv_time, axis=3), "mp")
    scaled = (
        conv_time
        * lax.rsqrt(square_sum / channels + 1e-06)[..., None]
        * norm_gain.astype(jnp.float32)
    )
    activated = jax.nn.silu(scaled).astype(jnp.bfloat16)
    weight_cut = spatial_weight
    conv_space = spatial_conv(lax.all_gather(activated, "mp", axis=3, tiled=True), weight_cut)
    latents = jnp.where(live_rows[:, None, None, None], conv_time + conv_space, 0.0).astype(
        jnp.bfloat16
    )
    return latents


CORES = 2
MIB = 1024 * 1024


def hop_order(hops):
    return [0] + sorted(range(1, hops), key=lambda k: (abs(k - hops // 2), k))


def lane_iota(shape):
    return lax.broadcasted_iota(jnp.int32, shape, len(shape) - 1)


def pick(index, table):
    out = jnp.zeros_like(index)
    for at, value in enumerate(table):
        out = jnp.where(index == at, value, out)
    return out


def partners(offset_ref, size, sign):
    rank = lax.axis_index("dp")
    return [lax.rem(rank + sign * offset_ref[j] + size, size) for j in range(size)]


def lane_of(rank, size, sign):
    me = lax.axis_index("dp")
    hops = size // 2
    hop = lax.rem(sign * (rank // 2 - me // 2) + hops, hops)
    at = jnp.int32(0)
    for index, value in enumerate(hop_order(hops)):
        at = jnp.where(hop == value, jnp.int32(index), at)
    return 2 * at + (rank + me) % 2


def pack_kernel(shifts, pair_rows, mark_dead, offset_ref, flag_ref, *refs):
    groups = flag_ref.shape[1]
    rows = groups * pair_rows
    levels = groups // shifts
    first = 0
    lanes = partners(offset_ref, shifts, 1)
    if mark_dead:
        own_ref, other_ref, joined = refs[0], refs[1], refs[-1]
        tokens, _, part, _ = joined.shape
        joined[:, 0] = own_ref[...].reshape(tokens, part, rows)
        joined[:, 1] = other_ref[...].reshape(tokens, part, rows)
        flat = joined.reshape(tokens * CORES * part, rows)
        levels = levels // CORES
        first = lax.axis_index("mp") % CORES * levels
        outs = refs[2:-1]
        lanes = [lane_of(rank, shifts, 1) for rank in lanes]
        lanes = [lane // 2 + lane % 2 * (shifts // 2) for lane in lanes]
    else:
        flat = refs[0]
        outs = refs[1:]
    slots = levels * pair_rows
    total = shifts * slots
    row = lane_iota((1, rows))
    place = pick(row // pair_rows % shifts, lanes)
    level = row // (pair_rows * shifts) - first
    target = place * slots + level * pair_rows + row % pair_rows
    target = jnp.where((level >= 0) & (level < levels), target, -1)
    hit = lax.broadcasted_iota(jnp.int32, (total, rows), 0) == target
    spread = (
        lax.broadcasted_iota(jnp.int32, (groups, rows), 0) == lane_iota((groups, rows)) // pair_rows
    ).astype(jnp.float32)
    flag = jnp.dot(flag_ref[...].astype(jnp.float32), spread, preferred_element_type=jnp.float32)
    if mark_dead:
        live = (row % pair_rows).astype(jnp.float32) < flag
        dead = jnp.sum(jnp.where(hit & jnp.logical_not(live), 1.0, 0.0), axis=1, keepdims=True) > 0.5
    else:
        hit = hit & (flag > 0.5)
    onehot = jnp.where(hit, 1.0, 0.0).astype(jnp.bfloat16)
    step = 512
    for start in range(0, flat.shape[0], step):
        tile = lax.dot_general(
            onehot,
            flat[start : start + step],
            (((1,), (1,)), ((), ())),
            preferred_element_type=jnp.float32,
        )
        if mark_dead:
            tile = jnp.where(dead, jnp.inf, tile)
        tile = tile.astype(jnp.bfloat16)
        begin = 0
        for out in outs:
            out[:, start : start + step] = tile[begin : begin + out.shape[0]]
            begin += out.shape[0]


def pack(shifts, pair_rows, mark_dead, offset, flag, *sources):
    height, rows = sources[0].shape
    total = rows // len(sources)
    width = height * len(sources)
    vmem = pl.BlockSpec(memory_space=pltpu.VMEM)
    scratch = []
    pieces = [total]
    if mark_dead:
        part = 64
        scratch = [pltpu.VMEM((height // part, CORES, part, rows), jnp.bfloat16)]
        pieces = [total // shifts] * (shifts // 2) + [total // 2]
    return pl.pallas_call(
        functools.partial(pack_kernel, shifts, pair_rows, mark_dead),
        out_shape=[jax.ShapeDtypeStruct((piece, width), jnp.bfloat16) for piece in pieces],
        in_specs=[pl.BlockSpec(memory_space=pltpu.SMEM)] + [vmem] * (1 + len(sources)),
        out_specs=[vmem] * len(pieces),
        scratch_shapes=scratch,
        compiler_params=pltpu.CompilerParams(vmem_limit_bytes=16 * MIB),
        cost_estimate=pl.CostEstimate(
            flops=2 * total * width * rows, bytes_accessed=2 * width * rows, transcendentals=0
        ),
        name="pack_dead" if mark_dead else "pack_carried",
    )(offset, flag, *sources)


def choose_kernel(shifts, pair_rows, group_offset_ref, cache_offset_ref, group_ref, *refs):
    near, far, near_other, far_other = refs[:4]
    outs = refs[4:]
    core = lax.axis_index("mp") % CORES
    groups = group_ref.shape[1]
    rows, width = near.shape
    slots = rows // shifts
    half_levels = groups // shifts // CORES
    column = lane_iota((1, rows))
    source = column // slots
    residue = jnp.zeros_like(column)
    for j, rank in enumerate(partners(cache_offset_ref, shifts, -1)):
        residue = jnp.where(source == rank, j, residue)
    cached = column % slots // pair_rows * shifts + residue
    pickers = (lax.broadcasted_iota(jnp.int32, (groups, rows), 0) == cached).astype(jnp.float32)
    group = jnp.dot(
        group_ref[...].astype(jnp.float32), pickers, preferred_element_type=jnp.float32
    )
    group = (group + 0.5).astype(jnp.int32)
    lanes = [lane_of(rank, shifts, -1) for rank in partners(group_offset_ref, shifts, -1)]
    place = pick(group % shifts, lanes)
    goal = group // shifts - core * half_levels
    half = rows // CORES
    target = (place * half_levels + goal) * pair_rows + column % pair_rows
    target = jnp.where((goal >= 0) & (goal < half_levels), target, -1)
    onehot = jnp.where(
        lax.broadcasted_iota(jnp.int32, (half, rows), 0) == target, 1.0, 0.0
    ).astype(jnp.bfloat16)
    step = 512
    part = 64
    piece = half // len(outs)
    for side, pair in enumerate(((near, near_other), (far, far_other))):
        for start in range(0, width, step):
            got = [
                jnp.dot(onehot, one[:, start : start + step], preferred_element_type=jnp.float32)
                for one in pair
            ]
            mixed = jnp.concatenate(
                [one[:, at : at + part] for at in range(0, step, part) for one in got], axis=1
            ).astype(jnp.bfloat16)
            lane = CORES * (side * width + start)
            for at, out in enumerate(outs):
                out[:, lane : lane + CORES * step] = mixed[at * piece : (at + 1) * piece]


def choose(shifts, pair_rows, pieces, group_offset, cache_offset, group, *sources):
    rows, width = sources[0].shape
    vmem = pl.BlockSpec(memory_space=pltpu.VMEM)
    smem = pl.BlockSpec(memory_space=pltpu.SMEM)
    total = len(sources) * width
    out = jax.ShapeDtypeStruct((rows // CORES // pieces, total), jnp.bfloat16)
    return pl.pallas_call(
        functools.partial(choose_kernel, shifts, pair_rows),
        out_shape=[out] * pieces,
        in_specs=[smem, smem] + [vmem] * (1 + len(sources)),
        out_specs=[vmem] * pieces,
        compiler_params=pltpu.CompilerParams(vmem_limit_bytes=16 * MIB),
        cost_estimate=pl.CostEstimate(
            flops=rows * rows * total, bytes_accessed=3 * rows * total, transcendentals=0
        ),
        name="choose_carried",
    )(group_offset, cache_offset, group, *sources)


def weights_kernel(taps, own, other, far, time_out, space_out, gain_out):
    index = lax.axis_index("mp")
    part = own.shape[1]
    height = far.shape[0] // 2
    inner = (height - 16) // taps
    side = inner // 4
    sources = ((own, 0), (other, 0), (far, 0), (far, height))
    for block, (ref, base) in enumerate(sources):
        columns = slice(block * part, (block + 1) * part)
        for tap in range(taps):
            for at in range(4):
                begin = pl.multiple_of(base + tap * inner + (index ^ at) * side, 16)
                rows = slice(tap * inner + at * side, tap * inner + (at + 1) * side)
                time_out[rows, columns] = ref[pl.ds(begin, side), :]
        gain_out[:, columns] = ref[base + taps * inner : base + height, :]
    channels = 4 * part
    for tap in range(3):
        for block in range(4):
            begin = pl.multiple_of(height + tap * channels + (index ^ block) * part, 16)
            rows = slice(tap * channels + block * part, tap * channels + (block + 1) * part)
            space_out[rows, :part] = own[pl.ds(begin, part), :]
            space_out[rows, part:] = other[pl.ds(begin, part), :]


def arrange_weights(taps, own, other, far):
    part = own.shape[1]
    height = far.shape[0] // 2
    vmem = pl.BlockSpec(memory_space=pltpu.VMEM)
    return pl.pallas_call(
        functools.partial(weights_kernel, taps),
        out_shape=[
            jax.ShapeDtypeStruct((height - 16, 4 * part), jnp.bfloat16),
            jax.ShapeDtypeStruct((own.shape[0] - height, 2 * part), jnp.bfloat16),
            jax.ShapeDtypeStruct((16, 4 * part), jnp.bfloat16),
        ],
        in_specs=[vmem] * 3,
        out_specs=[vmem] * 3,
        compiler_params=pltpu.CompilerParams(vmem_limit_bytes=12 * MIB),
        cost_estimate=pl.CostEstimate(
            flops=0, bytes_accessed=8 * own.size, transcendentals=0
        ),
        name="arrange_weights",
    )(own, other, far)


def encode_kernel(cuts, width, *refs):
    count = len(cuts[0]) + len(cuts[1])
    near, far = refs[: len(cuts[0])], refs[len(cuts[0]) : count]
    carried, time_w, space_w, gain_ref, kept, sent, seq, act, rest = refs[count:]
    rows = carried.shape[0]
    channels = time_w.shape[1]
    span = seq.shape[0]
    tokens = width * rows
    inner = near[0].shape[1] // (span * width) * 2
    side = inner // 2
    taps = time_w.shape[0] // inner
    half_width = carried.shape[1] // 2
    past = half_width // (side * width)

    def fill(step, rows_at, column, value):
        for t in range(span):
            tap = past + t - step
            if 0 <= tap < taps:
                seq[t, rows_at, tap * inner + column : tap * inner + column + side] = value

    for w in range(width):
        for step in range(past):
            lane = (step * width + w) * side
            for column, base in ((0, 0), (side, half_width)):
                value = carried[:, base + lane : base + lane + side]
                fill(step, slice(w * rows, (w + 1) * rows), column, value)
        for step in range(span):
            lane = (step * width + w) * side
            for column, sources, cut in ((0, near, cuts[0]), (side, far, cuts[1])):
                begin = w * rows
                for ref, (low, high) in zip(sources, cut):
                    value = ref[low:high, lane : lane + side]
                    fill(past + step, slice(begin, begin + high - low), column, value)
                    begin += high - low
    first = jnp.concatenate(
        [ref[a:b, :side].astype(jnp.float32)[:, :1] for ref, (a, b) in zip(near, cuts[0])], axis=0
    )
    live = (first < jnp.inf)[None]
    gain = gain_ref[0:1, :].astype(jnp.float32)
    kept_columns = space_w.shape[1]
    edge = jnp.zeros((rows, channels), jnp.bfloat16)
    for t in range(span):
        act[t, 0:rows, :channels] = edge
        act[t, tokens - rows :, 2 * channels :] = edge
    tile = 256
    for t in range(span):
        for start in range(0, tokens, tile):
            conv = jnp.dot(
                seq[t, start : start + tile], time_w[...], preferred_element_type=jnp.float32
            )
            square = jnp.sum(conv * conv, axis=1, keepdims=True)
            rest[t, start : start + tile] = conv[:, :kept_columns]
            scaled = conv * lax.rsqrt(square / channels + 1e-06) * gain
            value = jax.nn.silu(scaled).astype(jnp.bfloat16)
            act[t, start : start + tile, channels : 2 * channels] = value
            if start + tile < tokens:
                act[t, start + rows : start + rows + tile, :channels] = value
            else:
                act[t, start + rows : tokens, :channels] = value[: tile - rows]
            if start > 0:
                act[t, start - rows : start - rows + tile, 2 * channels :] = value
            else:
                act[t, : tile - rows, 2 * channels :] = value[rows:]
    tile = 256
    for t in range(span):
        for start in range(0, tokens, tile):
            total = rest[t, start : start + tile] + jnp.dot(
                act[t, start : start + tile], space_w[...], preferred_element_type=jnp.float32
            )
            wide = tile // rows
            total = jnp.where(live, total.reshape(wide, rows, kept_columns), 0.0)
            total = jnp.swapaxes(total, 0, 1).astype(jnp.bfloat16)
            place = slice(start // rows, start // rows + wide)
            kept[:, t, place] = total[:, :, : kept_columns // 2]
            sent[:, t, place] = total[:, :, kept_columns // 2 :]


def encode(width, span, near, far, carried, time_w, space_w, gain):
    cuts = [[(a, b) for _, a, b in pieces] for pieces in (near, far)]
    arrays = [x for pieces in (near, far) for x, _, _ in pieces]
    rows, lanes = carried.shape[0], arrays[0].shape[1]
    channels = time_w.shape[1]
    vmem = pl.BlockSpec(memory_space=pltpu.VMEM)
    part = space_w.shape[1] // 2
    out = jax.ShapeDtypeStruct((rows, span, width, part), jnp.bfloat16)
    tokens = rows * span * width
    return pl.pallas_call(
        functools.partial(encode_kernel, cuts, width),
        out_shape=[out, out],
        in_specs=[vmem] * (len(arrays) + 4),
        out_specs=[vmem] * 2,
        scratch_shapes=[
            pltpu.VMEM((span, width * rows, time_w.shape[0]), jnp.bfloat16),
            pltpu.VMEM((span, width * rows, space_w.shape[0]), jnp.bfloat16),
            pltpu.VMEM((span, width * rows, space_w.shape[1]), jnp.float32),
        ],
        compiler_params=pltpu.CompilerParams(vmem_limit_bytes=24 * MIB),
        cost_estimate=pl.CostEstimate(
            flops=2 * tokens * (time_w.size + space_w.size),
            bytes_accessed=2 * (time_w.size + space_w.size) + 16 * rows * lanes,
            transcendentals=tokens * channels,
        ),
        name="encode_rows",
    )(*arrays, carried, time_w, space_w, gain)


def place_kernel(shifts, offset_ref, *refs):
    blocks, out = refs[:-1], refs[-1]
    core = lax.axis_index("mp") % CORES
    lanes = [lane_of(rank, shifts, -1) for rank in partners(offset_ref, shifts, -1)]
    chunks = len(blocks) // 2
    for lane in range(shifts):
        residue = jnp.int32(0)
        for j in range(shifts):
            residue = jnp.where(lanes[j] == lane, jnp.int32(j), residue)
        for kind in range(2):
            out[core ^ kind, :, residue] = blocks[kind * chunks + lane // 2][lane % 2]


def place(shifts, pair_rows, offset, kept, got):
    rows, span, width, part = kept[0].shape
    half_levels = rows // 2 // pair_rows
    tail = (pair_rows, span, width, part)
    blocks = [a.reshape((2, half_levels) + tail) for a in kept + got]
    vmem = pl.BlockSpec(memory_space=pltpu.VMEM)
    out = pl.pallas_call(
        functools.partial(place_kernel, shifts),
        out_shape=jax.ShapeDtypeStruct((CORES, half_levels, shifts) + tail, jnp.bfloat16),
        in_specs=[pl.BlockSpec(memory_space=pltpu.SMEM)] + [vmem] * len(blocks),
        out_specs=vmem,
        compiler_params=pltpu.CompilerParams(vmem_limit_bytes=12 * MIB),
        cost_estimate=pl.CostEstimate(
            flops=0, bytes_accessed=4 * sum(a.size for a in blocks), transcendentals=0
        ),
        name="place_rows",
    )(offset, *blocks)
    return out.reshape((-1, span, width, part))


def routed_local(
    frames,
    cache,
    group_offset,
    cache_offset,
    cache_group,
    group_rows,
    cache_live,
    temporal_weight,
    spatial_weight,
    norm_gain,
):
    shifts = lax.axis_size("dp")
    parts = lax.axis_size("mp")
    groups = group_offset.shape[0]
    rows, span, width, part_in = frames.shape
    pair_rows = rows // groups
    taps = temporal_weight.shape[0]
    hops = shifts // 2

    def after(x, *cells):
        got = lax.optimization_barrier((x, *[cell[0] for cell in cells]))
        for cell, value in zip(cells, got[1:]):
            cell[0] = value
        return got[0]

    def flip(x, mask, *cells):
        x = after(x, *cells) if cells else x
        return [lax.ppermute(x, "mp", [(i, i ^ mask) for i in range(parts)])]

    def hop(x, distance, *cells):
        x = after(x, *cells) if cells else x
        return [lax.ppermute(x, "dp", [(i, (i + 2 * distance) % shifts) for i in range(shifts)])]

    cache_rows = cache.transpose((1, 2, 3, 0)).reshape((-1, rows))
    frame_rows = frames.transpose((1, 2, 3, 0)).reshape((-1, rows))
    (cache_packed,) = pack(
        shifts, pair_rows, False, cache_offset, cache_live.reshape((1, groups)), cache_rows
    )
    near = [lax.all_to_all(cache_packed, "dp", split_axis=0, concat_axis=0, tiled=True)]
    frame_swapped = flip(frame_rows, 1)
    *straight, crossing = pack(
        shifts,
        pair_rows,
        True,
        group_offset,
        group_rows.reshape((1, groups)),
        frame_rows,
        frame_swapped[0],
    )
    crossed = lax.ppermute(crossing, "dp", [(i, i ^ 1) for i in range(shifts)])
    slots = straight[0].shape[0]
    ready = [
        [jnp.concatenate([x, crossed[at * slots : (at + 1) * slots]], axis=0)]
        for at, x in enumerate(straight)
    ]
    first_far = flip(ready[0][0], 2)
    part = norm_gain.shape[0]
    time_rows = taps * temporal_weight.shape[1] + 16
    own_w = jnp.concatenate(
        [
            temporal_weight.reshape((-1, part)),
            jnp.broadcast_to(norm_gain[None], (16, part)),
            spatial_weight.reshape((-1, part)),
        ],
        axis=0,
    )
    other_w = flip(own_w, 1)
    far_w = flip(
        jnp.concatenate([own_w[:time_rows], other_w[0][:time_rows]], axis=0), 2
    )
    arranged = [[x] for x in arrange_weights(taps, own_w, other_w[0], far_w[0])]
    far = flip(near[0], 2, arranged[0], first_far)
    near_other = flip(near[0], 1, first_far)
    frame_near, frame_far = [ready[0]], [first_far]
    for at, distance in enumerate(hop_order(hops)[1:], 1):
        frame_near.append(hop(ready[at][0], distance, near))
    far_other = flip(far[0], 1, *frame_near[1:])
    carried = choose(
        shifts,
        pair_rows,
        hops,
        group_offset,
        cache_offset,
        cache_group.reshape((1, groups)),
        near[0],
        far[0],
        near_other[0],
        far_other[0],
    )
    frame_far += [flip(x[0], 2) for x in frame_near[1:]]
    kept, got = [], []
    for index in range(hops):
        ours = [(frame_near[index][0], 0, 2 * slots)]
        theirs = [(frame_far[index][0], 0, 2 * slots)]
        keep, give = encode(
            width, span, ours, theirs, carried[index], *[x[0] for x in arranged]
        )
        kept.append(keep)
        got.append(flip(give, 1)[0])
    return place(shifts, pair_rows, group_offset, kept, got)


def fits(mesh, frames, group_offset, temporal_weight):
    shifts, parts = mesh.shape["dp"], mesh.shape["mp"]
    groups = group_offset.shape[0]
    rows = frames.shape[0] // shifts
    if parts != 4 or frames.shape[3] != 64 * parts or groups > 256:
        return False
    if temporal_weight.shape[2] != 128 * parts or shifts % 2:
        return False
    if groups % (shifts * CORES):
        return False
    return rows // shifts // CORES % 16 == 0 and rows % 128 == 0


def solution(mesh):
    in_specs = (
        P("dp", None, None, "mp"),
        P("dp", None, None, "mp"),
        P(),
        P(),
        P(),
        P("dp", None),
        P("dp"),
        P(None, None, "mp"),
        P(None, None, "mp"),
        P("mp"),
    )
    out_specs = P("dp", None, None, "mp")

    def call(*args):
        body = routed_local if fits(mesh, args[0], args[2], args[7]) else plain_local
        return jax.shard_map(
            body, mesh=mesh, in_specs=in_specs, out_specs=out_specs, check_vma=False
        )(*args)

    return call
```

```python
import functools

import jax
import jax.numpy as jnp
from jax import lax
from jax.experimental import pallas as pl
from jax.experimental.pallas import tpu as pltpu
from jax.sharding import PartitionSpec as P


def temporal_conv(sequence, weight_part, span_steps):
    taps = weight_part.shape[0]
    windows = [
        sequence[:, taps - 1 - tap_index : taps - 1 - tap_index + span_steps]
        for tap_index in range(taps)
    ]
    joined = jnp.concatenate(windows, axis=3)
    flat_weight = weight_part.reshape((taps * weight_part.shape[1], weight_part.shape[2]))
    return jnp.einsum("rtwc,cd->rtwd", joined, flat_weight, preferred_element_type=jnp.float32)


def spatial_conv(activated, weight_part):
    width = activated.shape[2]
    padded = jnp.pad(activated, ((0, 0), (0, 0), (1, 1), (0, 0)))
    joined = jnp.concatenate(
        [padded[:, :, tap_index : tap_index + width] for tap_index in range(3)], axis=3
    )
    flat_weight = weight_part.reshape((3 * weight_part.shape[1], weight_part.shape[2]))
    return jnp.einsum("rtwc,cd->rtwd", joined, flat_weight, preferred_element_type=jnp.float32)


def to_slots(values, slot_index, owner_count, per_pair):
    buffer = (
        jnp.zeros((owner_count * per_pair,) + values.shape[1:], values.dtype)
        .at[slot_index]
        .set(values)
    )
    return buffer.reshape((owner_count, per_pair) + values.shape[1:])


def plain_local(
    frames,
    cache,
    group_offset,
    cache_offset,
    cache_group,
    group_rows,
    cache_live,
    temporal_weight,
    spatial_weight,
    norm_gain,
):
    owner_count = lax.axis_size("dp")
    my_rank = lax.axis_index("dp")
    groups = group_offset.shape[0]
    pair_rows = frames.shape[0] // groups
    span_steps = frames.shape[1]
    per_pair = (groups + owner_count - 1) // owner_count
    group_index = jnp.arange(groups, dtype=jnp.int32)
    slot_level = group_index // owner_count
    grouped = frames.reshape((groups, pair_rows) + frames.shape[1:])
    counts = group_rows.reshape(groups)
    send_slot = (my_rank + group_offset) % owner_count * per_pair + slot_level
    got_rows, got_counts = (
        lax.all_to_all(
            to_slots(grouped, send_slot, owner_count, per_pair),
            "dp",
            split_axis=0,
            concat_axis=0,
            tiled=True,
        ),
        lax.all_to_all(
            to_slots(counts, send_slot, owner_count, per_pair),
            "dp",
            split_axis=0,
            concat_axis=0,
            tiled=True,
        ),
    )
    take_slot = (my_rank - group_offset) % owner_count * per_pair + slot_level
    own_rows = got_rows.reshape((owner_count * per_pair,) + grouped.shape[1:])[take_slot]
    own_counts = got_counts.reshape(owner_count * per_pair)[take_slot]
    cache_grouped = cache.reshape((groups, pair_rows) + cache.shape[1:])
    cache_send = (my_rank + cache_offset) % owner_count * per_pair + slot_level
    got_cache, got_flags = (
        lax.all_to_all(
            to_slots(cache_grouped, cache_send, owner_count, per_pair),
            "dp",
            split_axis=0,
            concat_axis=0,
            tiled=True,
        ),
        lax.all_to_all(
            to_slots(cache_live, cache_send, owner_count, per_pair),
            "dp",
            split_axis=0,
            concat_axis=0,
            tiled=True,
        ),
    )
    inverse = jnp.sum(
        group_index[:, None] * (cache_group[:, None] == group_index[None, :]).astype(jnp.int32),
        axis=0,
    )
    cache_slot = (my_rank - cache_offset[inverse]) % owner_count * per_pair + inverse // owner_count
    own_cache = got_cache.reshape((owner_count * per_pair,) + cache_grouped.shape[1:])[cache_slot]
    own_flags = got_flags.reshape(owner_count * per_pair)[cache_slot]
    own_cache = jnp.where(
        own_flags[:, None, None, None, None] > 0, own_cache, jnp.zeros_like(own_cache)
    )
    sequence = jnp.concatenate([own_cache, own_rows], axis=2)
    sequence = sequence.reshape((groups * pair_rows,) + sequence.shape[2:])
    live_rows = (jnp.arange(pair_rows, dtype=jnp.int32)[None, :] < own_counts[:, None]).reshape(
        groups * pair_rows
    )
    channels = spatial_weight.shape[1]
    weight_cut = temporal_weight
    conv_time = temporal_conv(
        lax.all_gather(sequence, "mp", axis=3, tiled=True), weight_cut, span_steps
    )
    square_sum = lax.psum(jnp.sum(conv_time * conv_time, axis=3), "mp")
    scaled = (
        conv_time
        * lax.rsqrt(square_sum / channels + 1e-06)[..., None]
        * norm_gain.astype(jnp.float32)
    )
    activated = jax.nn.silu(scaled).astype(jnp.bfloat16)
    weight_cut = spatial_weight
    conv_space = spatial_conv(lax.all_gather(activated, "mp", axis=3, tiled=True), weight_cut)
    latents = jnp.where(live_rows[:, None, None, None], conv_time + conv_space, 0.0).astype(
        jnp.bfloat16
    )
    return latents


CORES = 2
MIB = 1024 * 1024
EARLY = (2,)


def hop_order(hops):
    return [0] + sorted(range(1, hops), key=lambda k: (abs(k - hops // 2), k))


def lane_iota(shape):
    return lax.broadcasted_iota(jnp.int32, shape, len(shape) - 1)


def pick(index, table):
    out = jnp.zeros_like(index)
    for at, value in enumerate(table):
        out = jnp.where(index == at, value, out)
    return out


def partners(offset_ref, size, sign):
    rank = lax.axis_index("dp")
    return [lax.rem(rank + sign * offset_ref[j] + size, size) for j in range(size)]


def lane_of(rank, size, sign):
    me = lax.axis_index("dp")
    hops = size // 2
    hop = lax.rem(sign * (rank // 2 - me // 2) + hops, hops)
    at = jnp.int32(0)
    for index, value in enumerate(hop_order(hops)):
        at = jnp.where(hop == value, jnp.int32(index), at)
    return 2 * at + (rank + me) % 2


def pack_kernel(shifts, pair_rows, mark_dead, offset_ref, flag_ref, *refs):
    groups = flag_ref.shape[1]
    rows = groups * pair_rows
    levels = groups // shifts
    first = 0
    lanes = partners(offset_ref, shifts, 1)
    if mark_dead:
        own_ref, other_ref, joined = refs[0], refs[1], refs[-1]
        tokens, _, part, _ = joined.shape
        joined[:, 0] = own_ref[...].reshape(tokens, part, rows)
        joined[:, 1] = other_ref[...].reshape(tokens, part, rows)
        flat = joined.reshape(tokens * CORES * part, rows)
        levels = levels // CORES
        first = lax.axis_index("mp") % CORES * levels
        outs = refs[2:-1]
        lanes = [lane_of(rank, shifts, 1) for rank in lanes]
        lanes = [lane // 2 + lane % 2 * (shifts // 2) for lane in lanes]
    else:
        flat = refs[0]
        outs = refs[1:]
    slots = levels * pair_rows
    total = shifts * slots
    row = lane_iota((1, rows))
    place = pick(row // pair_rows % shifts, lanes)
    level = row // (pair_rows * shifts) - first
    target = place * slots + level * pair_rows + row % pair_rows
    target = jnp.where((level >= 0) & (level < levels), target, -1)
    hit = lax.broadcasted_iota(jnp.int32, (total, rows), 0) == target
    spread = (
        lax.broadcasted_iota(jnp.int32, (groups, rows), 0) == lane_iota((groups, rows)) // pair_rows
    ).astype(jnp.float32)
    flag = jnp.dot(flag_ref[...].astype(jnp.float32), spread, preferred_element_type=jnp.float32)
    if mark_dead:
        live = (row % pair_rows).astype(jnp.float32) < flag
        dead = jnp.sum(jnp.where(hit & jnp.logical_not(live), 1.0, 0.0), axis=1, keepdims=True) > 0.5
    else:
        hit = hit & (flag > 0.5)
    onehot = jnp.where(hit, 1.0, 0.0).astype(jnp.bfloat16)
    step = 512
    for start in range(0, flat.shape[0], step):
        tile = lax.dot_general(
            onehot,
            flat[start : start + step],
            (((1,), (1,)), ((), ())),
            preferred_element_type=jnp.float32,
        )
        if mark_dead:
            tile = jnp.where(dead, jnp.inf, tile)
        tile = tile.astype(jnp.bfloat16)
        begin = 0
        for out in outs:
            out[:, start : start + step] = tile[begin : begin + out.shape[0]]
            begin += out.shape[0]


def pack(shifts, pair_rows, mark_dead, offset, flag, *sources):
    height, rows = sources[0].shape
    total = rows // len(sources)
    width = height * len(sources)
    vmem = pl.BlockSpec(memory_space=pltpu.VMEM)
    scratch = []
    pieces = [total]
    if mark_dead:
        part = 64
        scratch = [pltpu.VMEM((height // part, CORES, part, rows), jnp.bfloat16)]
        pieces = [total // shifts] * (shifts // 2) + [total // 2]
    return pl.pallas_call(
        functools.partial(pack_kernel, shifts, pair_rows, mark_dead),
        out_shape=[jax.ShapeDtypeStruct((piece, width), jnp.bfloat16) for piece in pieces],
        in_specs=[pl.BlockSpec(memory_space=pltpu.SMEM)] + [vmem] * (1 + len(sources)),
        out_specs=[vmem] * len(pieces),
        scratch_shapes=scratch,
        compiler_params=pltpu.CompilerParams(vmem_limit_bytes=16 * MIB),
        cost_estimate=pl.CostEstimate(
            flops=2 * total * width * rows, bytes_accessed=2 * width * rows, transcendentals=0
        ),
        name="pack_dead" if mark_dead else "pack_carried",
    )(offset, flag, *sources)


def choose_kernel(shifts, pair_rows, group_offset_ref, cache_offset_ref, group_ref, *refs):
    near, far, near_other, far_other = refs[:4]
    outs = refs[4:]
    core = lax.axis_index("mp") % CORES
    groups = group_ref.shape[1]
    rows, width = near.shape
    slots = rows // shifts
    half_levels = groups // shifts // CORES
    column = lane_iota((1, rows))
    source = column // slots
    residue = jnp.zeros_like(column)
    for j, rank in enumerate(partners(cache_offset_ref, shifts, -1)):
        residue = jnp.where(source == rank, j, residue)
    cached = column % slots // pair_rows * shifts + residue
    pickers = (lax.broadcasted_iota(jnp.int32, (groups, rows), 0) == cached).astype(jnp.float32)
    group = jnp.dot(
        group_ref[...].astype(jnp.float32), pickers, preferred_element_type=jnp.float32
    )
    group = (group + 0.5).astype(jnp.int32)
    lanes = [lane_of(rank, shifts, -1) for rank in partners(group_offset_ref, shifts, -1)]
    place = pick(group % shifts, lanes)
    goal = group // shifts - core * half_levels
    half = rows // CORES
    target = (place * half_levels + goal) * pair_rows + column % pair_rows
    target = jnp.where((goal >= 0) & (goal < half_levels), target, -1)
    onehot = jnp.where(
        lax.broadcasted_iota(jnp.int32, (half, rows), 0) == target, 1.0, 0.0
    ).astype(jnp.bfloat16)
    step = 512
    part = 64
    piece = half // len(outs)
    for side, pair in enumerate(((near, near_other), (far, far_other))):
        for start in range(0, width, step):
            got = [
                jnp.dot(onehot, one[:, start : start + step], preferred_element_type=jnp.float32)
                for one in pair
            ]
            mixed = jnp.concatenate(
                [one[:, at : at + part] for at in range(0, step, part) for one in got], axis=1
            ).astype(jnp.bfloat16)
            lane = CORES * (side * width + start)
            for at, out in enumerate(outs):
                out[:, lane : lane + CORES * step] = mixed[at * piece : (at + 1) * piece]


def choose(shifts, pair_rows, pieces, group_offset, cache_offset, group, *sources):
    rows, width = sources[0].shape
    vmem = pl.BlockSpec(memory_space=pltpu.VMEM)
    smem = pl.BlockSpec(memory_space=pltpu.SMEM)
    total = len(sources) * width
    out = jax.ShapeDtypeStruct((rows // CORES // pieces, total), jnp.bfloat16)
    return pl.pallas_call(
        functools.partial(choose_kernel, shifts, pair_rows),
        out_shape=[out] * pieces,
        in_specs=[smem, smem] + [vmem] * (1 + len(sources)),
        out_specs=[vmem] * pieces,
        compiler_params=pltpu.CompilerParams(vmem_limit_bytes=16 * MIB),
        cost_estimate=pl.CostEstimate(
            flops=rows * rows * total, bytes_accessed=3 * rows * total, transcendentals=0
        ),
        name="choose_carried",
    )(group_offset, cache_offset, group, *sources)


def weights_kernel(taps, own, other, far, time_out, space_out, gain_out):
    index = lax.axis_index("mp")
    part = own.shape[1]
    height = far.shape[0] // 2
    inner = (height - 16) // taps
    side = inner // 4
    sources = ((own, 0), (other, 0), (far, 0), (far, height))
    for block, (ref, base) in enumerate(sources):
        columns = slice(block * part, (block + 1) * part)
        for tap in range(taps):
            for at in range(4):
                begin = pl.multiple_of(base + tap * inner + (index ^ at) * side, 16)
                rows = slice(tap * inner + at * side, tap * inner + (at + 1) * side)
                time_out[rows, columns] = ref[pl.ds(begin, side), :]
        gain_out[:, columns] = ref[base + taps * inner : base + height, :]
    channels = 4 * part
    for tap in range(3):
        for block in range(4):
            begin = pl.multiple_of(height + tap * channels + (index ^ block) * part, 16)
            rows = slice(tap * channels + block * part, tap * channels + (block + 1) * part)
            space_out[rows, :part] = own[pl.ds(begin, part), :]
            space_out[rows, part:] = other[pl.ds(begin, part), :]


def arrange_weights(taps, own, other, far):
    part = own.shape[1]
    height = far.shape[0] // 2
    vmem = pl.BlockSpec(memory_space=pltpu.VMEM)
    return pl.pallas_call(
        functools.partial(weights_kernel, taps),
        out_shape=[
            jax.ShapeDtypeStruct((height - 16, 4 * part), jnp.bfloat16),
            jax.ShapeDtypeStruct((own.shape[0] - height, 2 * part), jnp.bfloat16),
            jax.ShapeDtypeStruct((16, 4 * part), jnp.bfloat16),
        ],
        in_specs=[vmem] * 3,
        out_specs=[vmem] * 3,
        compiler_params=pltpu.CompilerParams(vmem_limit_bytes=12 * MIB),
        cost_estimate=pl.CostEstimate(
            flops=0, bytes_accessed=8 * own.size, transcendentals=0
        ),
        name="arrange_weights",
    )(own, other, far)


def encode_kernel(cuts, width, *refs):
    count = len(cuts[0]) + len(cuts[1])
    near, far = refs[: len(cuts[0])], refs[len(cuts[0]) : count]
    carried, time_w, space_w, gain_ref, kept, sent, seq, act, rest = refs[count:]
    rows = carried.shape[0]
    channels = time_w.shape[1]
    span = seq.shape[0]
    tokens = width * rows
    inner = near[0].shape[1] // (span * width) * 2
    side = inner // 2
    taps = time_w.shape[0] // inner
    half_width = carried.shape[1] // 2
    past = half_width // (side * width)

    def fill(step, rows_at, column, value):
        for t in range(span):
            tap = past + t - step
            if 0 <= tap < taps:
                seq[t, rows_at, tap * inner + column : tap * inner + column + side] = value

    for w in range(width):
        for step in range(past):
            lane = (step * width + w) * side
            for column, base in ((0, 0), (side, half_width)):
                value = carried[:, base + lane : base + lane + side]
                fill(step, slice(w * rows, (w + 1) * rows), column, value)
        for step in range(span):
            lane = (step * width + w) * side
            for column, sources, cut in ((0, near, cuts[0]), (side, far, cuts[1])):
                begin = w * rows
                for ref, (low, high) in zip(sources, cut):
                    value = ref[low:high, lane : lane + side]
                    fill(past + step, slice(begin, begin + high - low), column, value)
                    begin += high - low
    first = jnp.concatenate(
        [ref[a:b, :side].astype(jnp.float32)[:, :1] for ref, (a, b) in zip(near, cuts[0])], axis=0
    )
    live = (first < jnp.inf)[None]
    gain = gain_ref[0:1, :].astype(jnp.float32)
    kept_columns = space_w.shape[1]
    edge = jnp.zeros((rows, channels), jnp.bfloat16)
    for t in range(span):
        act[t, 0:rows, :channels] = edge
        act[t, tokens - rows :, 2 * channels :] = edge
    tile = 256
    for t in range(span):
        for start in range(0, tokens, tile):
            conv = jnp.dot(
                seq[t, start : start + tile], time_w[...], preferred_element_type=jnp.float32
            )
            square = jnp.sum(conv * conv, axis=1, keepdims=True)
            rest[t, start : start + tile] = conv[:, :kept_columns]
            scaled = conv * lax.rsqrt(square / channels + 1e-06) * gain
            value = jax.nn.silu(scaled).astype(jnp.bfloat16)
            act[t, start : start + tile, channels : 2 * channels] = value
            if start + tile < tokens:
                act[t, start + rows : start + rows + tile, :channels] = value
            else:
                act[t, start + rows : tokens, :channels] = value[: tile - rows]
            if start > 0:
                act[t, start - rows : start - rows + tile, 2 * channels :] = value
            else:
                act[t, : tile - rows, 2 * channels :] = value[rows:]
    tile = 256
    for t in range(span):
        for start in range(0, tokens, tile):
            total = rest[t, start : start + tile] + jnp.dot(
                act[t, start : start + tile], space_w[...], preferred_element_type=jnp.float32
            )
            wide = tile // rows
            total = jnp.where(live, total.reshape(wide, rows, kept_columns), 0.0)
            total = jnp.swapaxes(total, 0, 1).astype(jnp.bfloat16)
            place = slice(start // rows, start // rows + wide)
            kept[:, t, place] = total[:, :, : kept_columns // 2]
            sent[:, t, place] = total[:, :, kept_columns // 2 :]


def encode(width, span, near, far, carried, time_w, space_w, gain):
    cuts = [[(a, b) for _, a, b in pieces] for pieces in (near, far)]
    arrays = [x for pieces in (near, far) for x, _, _ in pieces]
    rows, lanes = carried.shape[0], arrays[0].shape[1]
    channels = time_w.shape[1]
    vmem = pl.BlockSpec(memory_space=pltpu.VMEM)
    part = space_w.shape[1] // 2
    out = jax.ShapeDtypeStruct((rows, span, width, part), jnp.bfloat16)
    tokens = rows * span * width
    return pl.pallas_call(
        functools.partial(encode_kernel, cuts, width),
        out_shape=[out, out],
        in_specs=[vmem] * (len(arrays) + 4),
        out_specs=[vmem] * 2,
        scratch_shapes=[
            pltpu.VMEM((span, width * rows, time_w.shape[0]), jnp.bfloat16),
            pltpu.VMEM((span, width * rows, space_w.shape[0]), jnp.bfloat16),
            pltpu.VMEM((span, width * rows, space_w.shape[1]), jnp.float32),
        ],
        compiler_params=pltpu.CompilerParams(vmem_limit_bytes=24 * MIB),
        cost_estimate=pl.CostEstimate(
            flops=2 * tokens * (time_w.size + space_w.size),
            bytes_accessed=2 * (time_w.size + space_w.size) + 16 * rows * lanes,
            transcendentals=tokens * channels,
        ),
        name="encode_rows",
    )(*arrays, carried, time_w, space_w, gain)


def place_kernel(shifts, offset_ref, *refs):
    blocks, out = refs[:-1], refs[-1]
    core = lax.axis_index("mp") % CORES
    lanes = [lane_of(rank, shifts, -1) for rank in partners(offset_ref, shifts, -1)]
    chunks = len(blocks) // 2
    for lane in range(shifts):
        residue = jnp.int32(0)
        for j in range(shifts):
            residue = jnp.where(lanes[j] == lane, jnp.int32(j), residue)
        for kind in range(2):
            out[core ^ kind, :, residue] = blocks[kind * chunks + lane // 2][lane % 2]


def place(shifts, pair_rows, offset, kept, got):
    rows, span, width, part = kept[0].shape
    half_levels = rows // 2 // pair_rows
    tail = (pair_rows, span, width, part)
    blocks = [a.reshape((2, half_levels) + tail) for a in kept + got]
    vmem = pl.BlockSpec(memory_space=pltpu.VMEM)
    out = pl.pallas_call(
        functools.partial(place_kernel, shifts),
        out_shape=jax.ShapeDtypeStruct((CORES, half_levels, shifts) + tail, jnp.bfloat16),
        in_specs=[pl.BlockSpec(memory_space=pltpu.SMEM)] + [vmem] * len(blocks),
        out_specs=vmem,
        compiler_params=pltpu.CompilerParams(vmem_limit_bytes=12 * MIB),
        cost_estimate=pl.CostEstimate(
            flops=0, bytes_accessed=4 * sum(a.size for a in blocks), transcendentals=0
        ),
        name="place_rows",
    )(offset, *blocks)
    return out.reshape((-1, span, width, part))


def routed_local(
    frames,
    cache,
    group_offset,
    cache_offset,
    cache_group,
    group_rows,
    cache_live,
    temporal_weight,
    spatial_weight,
    norm_gain,
):
    shifts = lax.axis_size("dp")
    parts = lax.axis_size("mp")
    groups = group_offset.shape[0]
    rows, span, width, part_in = frames.shape
    pair_rows = rows // groups
    taps = temporal_weight.shape[0]
    hops = shifts // 2

    def after(x, *cells):
        got = lax.optimization_barrier((x, *[cell[0] for cell in cells]))
        for cell, value in zip(cells, got[1:]):
            cell[0] = value
        return got[0]

    def flip(x, mask, *cells):
        x = after(x, *cells) if cells else x
        return [lax.ppermute(x, "mp", [(i, i ^ mask) for i in range(parts)])]

    def hop(x, distance, *cells):
        x = after(x, *cells) if cells else x
        return [lax.ppermute(x, "dp", [(i, (i + 2 * distance) % shifts) for i in range(shifts)])]

    cache_rows = cache.transpose((1, 2, 3, 0)).reshape((-1, rows))
    frame_rows = frames.transpose((1, 2, 3, 0)).reshape((-1, rows))
    (cache_packed,) = pack(
        shifts, pair_rows, False, cache_offset, cache_live.reshape((1, groups)), cache_rows
    )
    near = [lax.all_to_all(cache_packed, "dp", split_axis=0, concat_axis=0, tiled=True)]
    frame_swapped = flip(frame_rows, 1)
    *straight, crossing = pack(
        shifts,
        pair_rows,
        True,
        group_offset,
        group_rows.reshape((1, groups)),
        frame_rows,
        frame_swapped[0],
    )
    crossed = lax.ppermute(crossing, "dp", [(i, i ^ 1) for i in range(shifts)])
    slots = straight[0].shape[0]
    ready = [
        [jnp.concatenate([x, crossed[at * slots : (at + 1) * slots]], axis=0)]
        for at, x in enumerate(straight)
    ]
    first_far = flip(ready[0][0], 2)
    part = norm_gain.shape[0]
    time_rows = taps * temporal_weight.shape[1] + 16
    own_w = jnp.concatenate(
        [
            temporal_weight.reshape((-1, part)),
            jnp.broadcast_to(norm_gain[None], (16, part)),
            spatial_weight.reshape((-1, part)),
        ],
        axis=0,
    )
    other_w = flip(own_w, 1)
    far_w = flip(
        jnp.concatenate([own_w[:time_rows], other_w[0][:time_rows]], axis=0), 2
    )
    arranged = [[x] for x in arrange_weights(taps, own_w, other_w[0], far_w[0])]
    early = {at: flip(ready[at][0], 2) for at in EARLY if at < hops}
    far = flip(near[0], 2, arranged[0], first_far, *early.values())
    near_other = flip(near[0], 1, first_far)
    frame_near, frame_far = [ready[0]], {0: first_far}
    for at, distance in enumerate(hop_order(hops)[1:], 1):
        frame_near.append(hop(ready[at][0], distance, near))
        if at in early:
            frame_far[at] = hop(early[at][0], distance, near)
    far_other = flip(far[0], 1, *frame_near[1:], *[frame_far[at] for at in early])
    carried = choose(
        shifts,
        pair_rows,
        hops,
        group_offset,
        cache_offset,
        cache_group.reshape((1, groups)),
        near[0],
        far[0],
        near_other[0],
        far_other[0],
    )
    for at in range(1, hops):
        if at not in early:
            frame_far[at] = flip(frame_near[at][0], 2)
    kept, got = [], []
    for index in range(hops):
        ours = [(frame_near[index][0], 0, 2 * slots)]
        theirs = [(frame_far[index][0], 0, 2 * slots)]
        keep, give = encode(
            width, span, ours, theirs, carried[index], *[x[0] for x in arranged]
        )
        kept.append(keep)
        got.append(flip(give, 1)[0])
    return place(shifts, pair_rows, group_offset, kept, got)


def fits(mesh, frames, group_offset, temporal_weight):
    shifts, parts = mesh.shape["dp"], mesh.shape["mp"]
    groups = group_offset.shape[0]
    rows = frames.shape[0] // shifts
    if parts != 4 or frames.shape[3] != 64 * parts or groups > 256:
        return False
    if temporal_weight.shape[2] != 128 * parts or shifts % 2:
        return False
    if groups % (shifts * CORES):
        return False
    return rows // shifts // CORES % 16 == 0 and rows % 128 == 0


def solution(mesh):
    in_specs = (
        P("dp", None, None, "mp"),
        P("dp", None, None, "mp"),
        P(),
        P(),
        P(),
        P("dp", None),
        P("dp"),
        P(None, None, "mp"),
        P(None, None, "mp"),
        P("mp"),
    )
    out_specs = P("dp", None, None, "mp")

    def call(*args):
        body = routed_local if fits(mesh, args[0], args[2], args[7]) else plain_local
        return jax.shard_map(
            body, mesh=mesh, in_specs=in_specs, out_specs=out_specs, check_vma=False
        )(*args)

    return call
```

```python
import functools

import jax
import jax.numpy as jnp
from jax import lax
from jax.experimental import pallas as pl
from jax.experimental.pallas import tpu as pltpu
from jax.sharding import PartitionSpec as P


def temporal_conv(sequence, weight_part, span_steps):
    taps = weight_part.shape[0]
    windows = [
        sequence[:, taps - 1 - tap_index : taps - 1 - tap_index + span_steps]
        for tap_index in range(taps)
    ]
    joined = jnp.concatenate(windows, axis=3)
    flat_weight = weight_part.reshape((taps * weight_part.shape[1], weight_part.shape[2]))
    return jnp.einsum("rtwc,cd->rtwd", joined, flat_weight, preferred_element_type=jnp.float32)


def spatial_conv(activated, weight_part):
    width = activated.shape[2]
    padded = jnp.pad(activated, ((0, 0), (0, 0), (1, 1), (0, 0)))
    joined = jnp.concatenate(
        [padded[:, :, tap_index : tap_index + width] for tap_index in range(3)], axis=3
    )
    flat_weight = weight_part.reshape((3 * weight_part.shape[1], weight_part.shape[2]))
    return jnp.einsum("rtwc,cd->rtwd", joined, flat_weight, preferred_element_type=jnp.float32)


def to_slots(values, slot_index, owner_count, per_pair):
    buffer = (
        jnp.zeros((owner_count * per_pair,) + values.shape[1:], values.dtype)
        .at[slot_index]
        .set(values)
    )
    return buffer.reshape((owner_count, per_pair) + values.shape[1:])


def plain_local(
    frames,
    cache,
    group_offset,
    cache_offset,
    cache_group,
    group_rows,
    cache_live,
    temporal_weight,
    spatial_weight,
    norm_gain,
):
    owner_count = lax.axis_size("dp")
    my_rank = lax.axis_index("dp")
    groups = group_offset.shape[0]
    pair_rows = frames.shape[0] // groups
    span_steps = frames.shape[1]
    per_pair = (groups + owner_count - 1) // owner_count
    group_index = jnp.arange(groups, dtype=jnp.int32)
    slot_level = group_index // owner_count
    grouped = frames.reshape((groups, pair_rows) + frames.shape[1:])
    counts = group_rows.reshape(groups)
    send_slot = (my_rank + group_offset) % owner_count * per_pair + slot_level
    got_rows, got_counts = (
        lax.all_to_all(
            to_slots(grouped, send_slot, owner_count, per_pair),
            "dp",
            split_axis=0,
            concat_axis=0,
            tiled=True,
        ),
        lax.all_to_all(
            to_slots(counts, send_slot, owner_count, per_pair),
            "dp",
            split_axis=0,
            concat_axis=0,
            tiled=True,
        ),
    )
    take_slot = (my_rank - group_offset) % owner_count * per_pair + slot_level
    own_rows = got_rows.reshape((owner_count * per_pair,) + grouped.shape[1:])[take_slot]
    own_counts = got_counts.reshape(owner_count * per_pair)[take_slot]
    cache_grouped = cache.reshape((groups, pair_rows) + cache.shape[1:])
    cache_send = (my_rank + cache_offset) % owner_count * per_pair + slot_level
    got_cache, got_flags = (
        lax.all_to_all(
            to_slots(cache_grouped, cache_send, owner_count, per_pair),
            "dp",
            split_axis=0,
            concat_axis=0,
            tiled=True,
        ),
        lax.all_to_all(
            to_slots(cache_live, cache_send, owner_count, per_pair),
            "dp",
            split_axis=0,
            concat_axis=0,
            tiled=True,
        ),
    )
    inverse = jnp.sum(
        group_index[:, None] * (cache_group[:, None] == group_index[None, :]).astype(jnp.int32),
        axis=0,
    )
    cache_slot = (my_rank - cache_offset[inverse]) % owner_count * per_pair + inverse // owner_count
    own_cache = got_cache.reshape((owner_count * per_pair,) + cache_grouped.shape[1:])[cache_slot]
    own_flags = got_flags.reshape(owner_count * per_pair)[cache_slot]
    own_cache = jnp.where(
        own_flags[:, None, None, None, None] > 0, own_cache, jnp.zeros_like(own_cache)
    )
    sequence = jnp.concatenate([own_cache, own_rows], axis=2)
    sequence = sequence.reshape((groups * pair_rows,) + sequence.shape[2:])
    live_rows = (jnp.arange(pair_rows, dtype=jnp.int32)[None, :] < own_counts[:, None]).reshape(
        groups * pair_rows
    )
    channels = spatial_weight.shape[1]
    weight_cut = temporal_weight
    conv_time = temporal_conv(
        lax.all_gather(sequence, "mp", axis=3, tiled=True), weight_cut, span_steps
    )
    square_sum = lax.psum(jnp.sum(conv_time * conv_time, axis=3), "mp")
    scaled = (
        conv_time
        * lax.rsqrt(square_sum / channels + 1e-06)[..., None]
        * norm_gain.astype(jnp.float32)
    )
    activated = jax.nn.silu(scaled).astype(jnp.bfloat16)
    weight_cut = spatial_weight
    conv_space = spatial_conv(lax.all_gather(activated, "mp", axis=3, tiled=True), weight_cut)
    latents = jnp.where(live_rows[:, None, None, None], conv_time + conv_space, 0.0).astype(
        jnp.bfloat16
    )
    return latents


CORES = 2
MIB = 1024 * 1024
EARLY = (2,)


def hop_order(hops):
    return [0] + sorted(range(1, hops), key=lambda k: (abs(k - hops // 2), k))


def lane_iota(shape):
    return lax.broadcasted_iota(jnp.int32, shape, len(shape) - 1)


def pick(index, table):
    out = jnp.zeros_like(index)
    for at, value in enumerate(table):
        out = jnp.where(index == at, value, out)
    return out


def partners(offset_ref, size, sign):
    rank = lax.axis_index("dp")
    return [lax.rem(rank + sign * offset_ref[j] + size, size) for j in range(size)]


def lane_of(rank, size, sign):
    me = lax.axis_index("dp")
    hops = size // 2
    hop = lax.rem(sign * (rank // 2 - me // 2) + hops, hops)
    at = jnp.int32(0)
    for index, value in enumerate(hop_order(hops)):
        at = jnp.where(hop == value, jnp.int32(index), at)
    return 2 * at + (rank + me) % 2


def pack_kernel(shifts, pair_rows, mark_dead, offset_ref, flag_ref, *refs):
    groups = flag_ref.shape[1]
    rows = groups * pair_rows
    levels = groups // shifts
    first = 0
    lanes = partners(offset_ref, shifts, 1)
    if mark_dead:
        own_ref, other_ref, joined = refs[0], refs[1], refs[-1]
        tokens, _, part, _ = joined.shape
        joined[:, 0] = own_ref[...].reshape(tokens, part, rows)
        joined[:, 1] = other_ref[...].reshape(tokens, part, rows)
        flat = joined.reshape(tokens * CORES * part, rows)
        levels = levels // CORES
        first = lax.axis_index("mp") % CORES * levels
        outs = refs[2:-1]
        lanes = [lane_of(rank, shifts, 1) for rank in lanes]
        lanes = [lane // 2 + lane % 2 * (shifts // 2) for lane in lanes]
    else:
        flat = refs[0]
        outs = refs[1:]
    slots = levels * pair_rows
    total = shifts * slots
    row = lane_iota((1, rows))
    place = pick(row // pair_rows % shifts, lanes)
    level = row // (pair_rows * shifts) - first
    target = place * slots + level * pair_rows + row % pair_rows
    target = jnp.where((level >= 0) & (level < levels), target, -1)
    hit = lax.broadcasted_iota(jnp.int32, (total, rows), 0) == target
    spread = (
        lax.broadcasted_iota(jnp.int32, (groups, rows), 0) == lane_iota((groups, rows)) // pair_rows
    ).astype(jnp.float32)
    flag = jnp.dot(flag_ref[...].astype(jnp.float32), spread, preferred_element_type=jnp.float32)
    if mark_dead:
        live = (row % pair_rows).astype(jnp.float32) < flag
        dead = jnp.sum(jnp.where(hit & jnp.logical_not(live), 1.0, 0.0), axis=1, keepdims=True) > 0.5
    else:
        hit = hit & (flag > 0.5)
    onehot = jnp.where(hit, 1.0, 0.0).astype(jnp.bfloat16)
    step = 512
    for start in range(0, flat.shape[0], step):
        tile = lax.dot_general(
            onehot,
            flat[start : start + step],
            (((1,), (1,)), ((), ())),
            preferred_element_type=jnp.float32,
        )
        if mark_dead:
            tile = jnp.where(dead, jnp.inf, tile)
        tile = tile.astype(jnp.bfloat16)
        begin = 0
        for out in outs:
            out[:, start : start + step] = tile[begin : begin + out.shape[0]]
            begin += out.shape[0]


def pack(shifts, pair_rows, mark_dead, offset, flag, *sources):
    height, rows = sources[0].shape
    total = rows // len(sources)
    width = height * len(sources)
    vmem = pl.BlockSpec(memory_space=pltpu.VMEM)
    scratch = []
    pieces = [total]
    if mark_dead:
        part = 64
        scratch = [pltpu.VMEM((height // part, CORES, part, rows), jnp.bfloat16)]
        pieces = [total // shifts] * (shifts // 2) + [total // 2]
    return pl.pallas_call(
        functools.partial(pack_kernel, shifts, pair_rows, mark_dead),
        out_shape=[jax.ShapeDtypeStruct((piece, width), jnp.bfloat16) for piece in pieces],
        in_specs=[pl.BlockSpec(memory_space=pltpu.SMEM)] + [vmem] * (1 + len(sources)),
        out_specs=[vmem] * len(pieces),
        scratch_shapes=scratch,
        compiler_params=pltpu.CompilerParams(vmem_limit_bytes=16 * MIB),
        cost_estimate=pl.CostEstimate(
            flops=2 * total * width * rows, bytes_accessed=2 * width * rows, transcendentals=0
        ),
        name="pack_dead" if mark_dead else "pack_carried",
    )(offset, flag, *sources)


def choose_kernel(shifts, pair_rows, group_offset_ref, cache_offset_ref, group_ref, *refs):
    near, far, near_other, far_other = refs[:4]
    outs = refs[4:]
    core = lax.axis_index("mp") % CORES
    groups = group_ref.shape[1]
    rows, width = near.shape
    slots = rows // shifts
    half_levels = groups // shifts // CORES
    column = lane_iota((1, rows))
    source = column // slots
    residue = jnp.zeros_like(column)
    for j, rank in enumerate(partners(cache_offset_ref, shifts, -1)):
        residue = jnp.where(source == rank, j, residue)
    cached = column % slots // pair_rows * shifts + residue
    pickers = (lax.broadcasted_iota(jnp.int32, (groups, rows), 0) == cached).astype(jnp.float32)
    group = jnp.dot(
        group_ref[...].astype(jnp.float32), pickers, preferred_element_type=jnp.float32
    )
    group = (group + 0.5).astype(jnp.int32)
    lanes = [lane_of(rank, shifts, -1) for rank in partners(group_offset_ref, shifts, -1)]
    place = pick(group % shifts, lanes)
    goal = group // shifts - core * half_levels
    half = rows // CORES
    target = (place * half_levels + goal) * pair_rows + column % pair_rows
    target = jnp.where((goal >= 0) & (goal < half_levels), target, -1)
    onehot = jnp.where(
        lax.broadcasted_iota(jnp.int32, (half, rows), 0) == target, 1.0, 0.0
    ).astype(jnp.bfloat16)
    step = 512
    part = 64
    piece = half // len(outs)
    for side, pair in enumerate(((near, near_other), (far, far_other))):
        for start in range(0, width, step):
            got = [
                jnp.dot(onehot, one[:, start : start + step], preferred_element_type=jnp.float32)
                for one in pair
            ]
            mixed = jnp.concatenate(
                [one[:, at : at + part] for at in range(0, step, part) for one in got], axis=1
            ).astype(jnp.bfloat16)
            lane = CORES * (side * width + start)
            for at, out in enumerate(outs):
                out[:, lane : lane + CORES * step] = mixed[at * piece : (at + 1) * piece]


def choose(shifts, pair_rows, pieces, group_offset, cache_offset, group, *sources):
    rows, width = sources[0].shape
    vmem = pl.BlockSpec(memory_space=pltpu.VMEM)
    smem = pl.BlockSpec(memory_space=pltpu.SMEM)
    total = len(sources) * width
    out = jax.ShapeDtypeStruct((rows // CORES // pieces, total), jnp.bfloat16)
    return pl.pallas_call(
        functools.partial(choose_kernel, shifts, pair_rows),
        out_shape=[out] * pieces,
        in_specs=[smem, smem] + [vmem] * (1 + len(sources)),
        out_specs=[vmem] * pieces,
        compiler_params=pltpu.CompilerParams(vmem_limit_bytes=16 * MIB),
        cost_estimate=pl.CostEstimate(
            flops=rows * rows * total, bytes_accessed=3 * rows * total, transcendentals=0
        ),
        name="choose_carried",
    )(group_offset, cache_offset, group, *sources)


def weights_kernel(taps, own, other, far, time_out, space_out, gain_out):
    index = lax.axis_index("mp")
    part = own.shape[1]
    height = far.shape[0] // 2
    inner = (height - 16) // taps
    side = inner // 4
    sources = ((own, 0), (other, 0), (far, 0), (far, height))
    for block, (ref, base) in enumerate(sources):
        columns = slice(block * part, (block + 1) * part)
        for tap in range(taps):
            for at in range(4):
                begin = pl.multiple_of(base + tap * inner + (index ^ at) * side, 16)
                rows = slice(tap * inner + at * side, tap * inner + (at + 1) * side)
                time_out[rows, columns] = ref[pl.ds(begin, side), :]
        gain_out[:, columns] = ref[base + taps * inner : base + height, :]
    channels = 4 * part
    for tap in range(3):
        for block in range(4):
            begin = pl.multiple_of(height + tap * channels + (index ^ block) * part, 16)
            rows = slice(tap * channels + block * part, tap * channels + (block + 1) * part)
            space_out[rows, :part] = own[pl.ds(begin, part), :]
            space_out[rows, part:] = other[pl.ds(begin, part), :]


def arrange_weights(taps, own, other, far):
    part = own.shape[1]
    height = far.shape[0] // 2
    vmem = pl.BlockSpec(memory_space=pltpu.VMEM)
    return pl.pallas_call(
        functools.partial(weights_kernel, taps),
        out_shape=[
            jax.ShapeDtypeStruct((height - 16, 4 * part), jnp.bfloat16),
            jax.ShapeDtypeStruct((own.shape[0] - height, 2 * part), jnp.bfloat16),
            jax.ShapeDtypeStruct((16, 4 * part), jnp.bfloat16),
        ],
        in_specs=[vmem] * 3,
        out_specs=[vmem] * 3,
        compiler_params=pltpu.CompilerParams(vmem_limit_bytes=12 * MIB),
        cost_estimate=pl.CostEstimate(
            flops=0, bytes_accessed=8 * own.size, transcendentals=0
        ),
        name="arrange_weights",
    )(own, other, far)


def encode_kernel(cuts, width, *refs):
    count = len(cuts[0]) + len(cuts[1])
    near, far = refs[: len(cuts[0])], refs[len(cuts[0]) : count]
    carried, time_w, space_w, gain_ref, kept, sent, seq, act, rest = refs[count:]
    rows = carried.shape[0]
    channels = time_w.shape[1]
    span = seq.shape[0]
    tokens = width * rows
    inner = near[0].shape[1] // (span * width) * 2
    side = inner // 2
    taps = time_w.shape[0] // inner
    half_width = carried.shape[1] // 2
    past = half_width // (side * width)

    def fill(step, rows_at, column, value):
        for t in range(span):
            tap = past + t - step
            if 0 <= tap < taps:
                seq[t, rows_at, tap * inner + column : tap * inner + column + side] = value

    for w in range(width):
        for step in range(past):
            lane = (step * width + w) * side
            for column, base in ((0, 0), (side, half_width)):
                value = carried[:, base + lane : base + lane + side]
                fill(step, slice(w * rows, (w + 1) * rows), column, value)
        for step in range(span):
            lane = (step * width + w) * side
            for column, sources, cut in ((0, near, cuts[0]), (side, far, cuts[1])):
                begin = w * rows
                for ref, (low, high) in zip(sources, cut):
                    value = ref[low:high, lane : lane + side]
                    fill(past + step, slice(begin, begin + high - low), column, value)
                    begin += high - low
    first = jnp.concatenate(
        [ref[a:b, :side].astype(jnp.float32)[:, :1] for ref, (a, b) in zip(near, cuts[0])], axis=0
    )
    live = (first < jnp.inf)[None]
    gain = gain_ref[0:1, :].astype(jnp.float32)
    kept_columns = space_w.shape[1]
    edge = jnp.zeros((rows, channels), jnp.bfloat16)
    for t in range(span):
        act[t, 0:rows, :channels] = edge
        act[t, tokens - rows :, 2 * channels :] = edge
    tile = 256
    for t in range(span):
        for start in range(0, tokens, tile):
            conv = jnp.dot(
                seq[t, start : start + tile], time_w[...], preferred_element_type=jnp.float32
            )
            square = jnp.sum(conv * conv, axis=1, keepdims=True)
            rest[t, start : start + tile] = conv[:, :kept_columns]
            scaled = conv * lax.rsqrt(square / channels + 1e-06) * gain
            value = jax.nn.silu(scaled).astype(jnp.bfloat16)
            act[t, start : start + tile, channels : 2 * channels] = value
            if start + tile < tokens:
                act[t, start + rows : start + rows + tile, :channels] = value
            else:
                act[t, start + rows : tokens, :channels] = value[: tile - rows]
            if start > 0:
                act[t, start - rows : start - rows + tile, 2 * channels :] = value
            else:
                act[t, : tile - rows, 2 * channels :] = value[rows:]
    tile = 256
    for t in range(span):
        for start in range(0, tokens, tile):
            total = rest[t, start : start + tile] + jnp.dot(
                act[t, start : start + tile], space_w[...], preferred_element_type=jnp.float32
            )
            wide = tile // rows
            total = jnp.where(live, total.reshape(wide, rows, kept_columns), 0.0)
            total = jnp.swapaxes(total, 0, 1).astype(jnp.bfloat16)
            place = slice(start // rows, start // rows + wide)
            kept[:, t, place] = total[:, :, : kept_columns // 2]
            sent[:, t, place] = total[:, :, kept_columns // 2 :]


def encode(width, span, near, far, carried, time_w, space_w, gain):
    cuts = [[(a, b) for _, a, b in pieces] for pieces in (near, far)]
    arrays = [x for pieces in (near, far) for x, _, _ in pieces]
    rows, lanes = carried.shape[0], arrays[0].shape[1]
    channels = time_w.shape[1]
    vmem = pl.BlockSpec(memory_space=pltpu.VMEM)
    part = space_w.shape[1] // 2
    out = jax.ShapeDtypeStruct((rows, span, width, part), jnp.bfloat16)
    tokens = rows * span * width
    return pl.pallas_call(
        functools.partial(encode_kernel, cuts, width),
        out_shape=[out, out],
        in_specs=[vmem] * (len(arrays) + 4),
        out_specs=[vmem] * 2,
        scratch_shapes=[
            pltpu.VMEM((span, width * rows, time_w.shape[0]), jnp.bfloat16),
            pltpu.VMEM((span, width * rows, space_w.shape[0]), jnp.bfloat16),
            pltpu.VMEM((span, width * rows, space_w.shape[1]), jnp.float32),
        ],
        compiler_params=pltpu.CompilerParams(vmem_limit_bytes=24 * MIB),
        cost_estimate=pl.CostEstimate(
            flops=2 * tokens * (time_w.size + space_w.size),
            bytes_accessed=2 * (time_w.size + space_w.size) + 16 * rows * lanes,
            transcendentals=tokens * channels,
        ),
        name="encode_rows",
    )(*arrays, carried, time_w, space_w, gain)


def place_kernel(shifts, offset_ref, *refs):
    blocks, out = refs[:-1], refs[-1]
    core = lax.axis_index("mp") % CORES
    lanes = [lane_of(rank, shifts, -1) for rank in partners(offset_ref, shifts, -1)]
    chunks = len(blocks) // 2
    for lane in range(shifts):
        residue = jnp.int32(0)
        for j in range(shifts):
            residue = jnp.where(lanes[j] == lane, jnp.int32(j), residue)
        for kind in range(2):
            out[core ^ kind, :, residue] = blocks[kind * chunks + lane // 2][lane % 2]


def place(shifts, pair_rows, offset, kept, got):
    rows, span, width, part = kept[0].shape
    half_levels = rows // 2 // pair_rows
    tail = (pair_rows, span, width, part)
    blocks = [a.reshape((2, half_levels) + tail) for a in kept + got]
    vmem = pl.BlockSpec(memory_space=pltpu.VMEM)
    out = pl.pallas_call(
        functools.partial(place_kernel, shifts),
        out_shape=jax.ShapeDtypeStruct((CORES, half_levels, shifts) + tail, jnp.bfloat16),
        in_specs=[pl.BlockSpec(memory_space=pltpu.SMEM)] + [vmem] * len(blocks),
        out_specs=vmem,
        compiler_params=pltpu.CompilerParams(vmem_limit_bytes=12 * MIB),
        cost_estimate=pl.CostEstimate(
            flops=0, bytes_accessed=4 * sum(a.size for a in blocks), transcendentals=0
        ),
        name="place_rows",
    )(offset, *blocks)
    return out.reshape((-1, span, width, part))


def routed_local(
    frames,
    cache,
    group_offset,
    cache_offset,
    cache_group,
    group_rows,
    cache_live,
    temporal_weight,
    spatial_weight,
    norm_gain,
):
    shifts = lax.axis_size("dp")
    parts = lax.axis_size("mp")
    groups = group_offset.shape[0]
    rows, span, width, part_in = frames.shape
    pair_rows = rows // groups
    taps = temporal_weight.shape[0]
    hops = shifts // 2

    def after(x, *cells):
        got = lax.optimization_barrier((x, *[cell[0] for cell in cells]))
        for cell, value in zip(cells, got[1:]):
            cell[0] = value
        return got[0]

    def flip(x, mask, *cells):
        x = after(x, *cells) if cells else x
        return [lax.ppermute(x, "mp", [(i, i ^ mask) for i in range(parts)])]

    def hop(x, distance, *cells):
        x = after(x, *cells) if cells else x
        return [lax.ppermute(x, "dp", [(i, (i + 2 * distance) % shifts) for i in range(shifts)])]

    cache_rows = cache.transpose((1, 2, 3, 0)).reshape((-1, rows))
    frame_rows = frames.transpose((1, 2, 3, 0)).reshape((-1, rows))
    (cache_packed,) = pack(
        shifts, pair_rows, False, cache_offset, cache_live.reshape((1, groups)), cache_rows
    )
    near = [lax.all_to_all(cache_packed, "dp", split_axis=0, concat_axis=0, tiled=True)]
    frame_swapped = flip(frame_rows, 1)
    *straight, crossing = pack(
        shifts,
        pair_rows,
        True,
        group_offset,
        group_rows.reshape((1, groups)),
        frame_rows,
        frame_swapped[0],
    )
    crossed = lax.ppermute(crossing, "dp", [(i, i ^ 1) for i in range(shifts)])
    slots = straight[0].shape[0]
    ready = [
        [jnp.concatenate([x, crossed[at * slots : (at + 1) * slots]], axis=0)]
        for at, x in enumerate(straight)
    ]
    first_far = flip(ready[0][0], 2)
    part = norm_gain.shape[0]
    time_rows = taps * temporal_weight.shape[1] + 16
    own_w = jnp.concatenate(
        [
            temporal_weight.reshape((-1, part)),
            jnp.broadcast_to(norm_gain[None], (16, part)),
            spatial_weight.reshape((-1, part)),
        ],
        axis=0,
    )
    other_w = flip(own_w, 1)
    far_w = flip(
        jnp.concatenate([own_w[:time_rows], other_w[0][:time_rows]], axis=0), 2
    )
    arranged = [[x] for x in arrange_weights(taps, own_w, other_w[0], far_w[0])]
    early = {at: flip(ready[at][0], 2) for at in EARLY if at < hops}
    far = flip(near[0], 2, arranged[0], first_far, *early.values())
    near_other = flip(near[0], 1, first_far)
    frame_near, frame_far = [ready[0]], {0: first_far}
    for at, distance in enumerate(hop_order(hops)[1:], 1):
        frame_near.append(hop(ready[at][0], distance, near if at == 1 else first_far))
        if at in early:
            frame_far[at] = hop(early[at][0], distance, near)
    far_other = flip(far[0], 1, *frame_near[1:], *[frame_far[at] for at in early])
    carried = choose(
        shifts,
        pair_rows,
        hops,
        group_offset,
        cache_offset,
        cache_group.reshape((1, groups)),
        near[0],
        far[0],
        near_other[0],
        far_other[0],
    )
    for at in range(1, hops):
        if at not in early:
            frame_far[at] = flip(frame_near[at][0], 2)
    kept, got = [], []
    for index in range(hops):
        ours = [(frame_near[index][0], 0, 2 * slots)]
        theirs = [(frame_far[index][0], 0, 2 * slots)]
        keep, give = encode(
            width, span, ours, theirs, carried[index], *[x[0] for x in arranged]
        )
        kept.append(keep)
        got.append(flip(give, 1)[0])
    return place(shifts, pair_rows, group_offset, kept, got)


def fits(mesh, frames, group_offset, temporal_weight):
    shifts, parts = mesh.shape["dp"], mesh.shape["mp"]
    groups = group_offset.shape[0]
    rows = frames.shape[0] // shifts
    if parts != 4 or frames.shape[3] != 64 * parts or groups > 256:
        return False
    if temporal_weight.shape[2] != 128 * parts or shifts % 2:
        return False
    if groups % (shifts * CORES):
        return False
    return rows // shifts // CORES % 16 == 0 and rows % 128 == 0


def solution(mesh):
    in_specs = (
        P("dp", None, None, "mp"),
        P("dp", None, None, "mp"),
        P(),
        P(),
        P(),
        P("dp", None),
        P("dp"),
        P(None, None, "mp"),
        P(None, None, "mp"),
        P("mp"),
    )
    out_specs = P("dp", None, None, "mp")

    def call(*args):
        body = routed_local if fits(mesh, args[0], args[2], args[7]) else plain_local
        return jax.shard_map(
            body, mesh=mesh, in_specs=in_specs, out_specs=out_specs, check_vma=False
        )(*args)

    return call
```
